128 devices in a mesh: ctx: 32 (over x, y, core), head: 4 (over z).
Axes of the slice: x: 4, y: 4, z: 4, core: 2. Of those that a mesh axis runs over, the one named last changes fastest.
Arguments:
- queries: bfloat16 [128, 4, 2048], P(None, 'head'), may hold values from -160 to 160, as said below
- key_codes: int32 [4, 128, 8, 32768], P('head', None, None, 'ctx'), may hold values from 0 to 255, as said below
- value_codes: int32 [4, 128, 8, 32768], P('head', None, None, 'ctx'), may hold values from 0 to 255
- key_book: bfloat16 [4, 8, 256, 16], P('head'), may hold values from -4 to 4
- value_book: bfloat16 [4, 8, 256, 16], P('head'), may hold values from -4 to 4
- lengths: int32 [128], replicated, may hold values from 1 to 32768, as said below
- resid: bfloat16 [128, 4096], P(None, 'ctx'), may hold values from -70 to 70
- w_out: bfloat16 [4, 2048, 4096], P('head', None, 'ctx'), may hold values from -2.5 to 2.5
- norm_gain: bfloat16 [4096], P('ctx'), may hold values from 0.25 to 1.75
- routes: int32 [128, 8], replicated, may hold values from 0 to 127, all different within a row; in each aligned block of 128 rows (0 to 127, 128 to 255, ...) at most 16 rows name the same one
- route_weights: float32 [128, 8], replicated, may hold values from 0.1 to 1
- w_gate: bfloat16 [128, 4096, 768], P(('ctx', 'head')), may hold values from -0.09375 to 0.09375
- w_up: bfloat16 [128, 4096, 768], P(('ctx', 'head')), may hold values from -0.09375 to 0.09375
- w_down: bfloat16 [128, 768, 4096], P(('ctx', 'head')), may hold values from -0.21875 to 0.21875
Outputs:
- layer_out: bfloat16 [128, 4096], P('head', 'ctx')
The draws below stay inside these ranges and needn't reach their ends.
Inputs may be any that keep to these rules, and one draw needn't show every extreme that they name: `queries`: query rows of a few draws may be far larger than others. `key_codes`: at positions p with p mod 64 equal to 5 every code is 0; at p mod 64 equal to 9 subvector 0 has code 1 and the others 0. `lengths`: some row has length 32768. `routes`: each row names 8 different experts; no expert is named by more than 16 rows, and one is named by exactly 16; every expert is named by some row.
All inputs are finite; a program needn't handle non-finite values.
Results may differ from the reference program's by a relative error of at most 0.007.
Values may be sent and summed in bfloat16 or wider, within the bound.
A program may use at most 192 MiB of HBM per device.

```python
import math
import jax
import jax.numpy as jnp
import numpy as np
from jax import lax

D = 4096
QH = 16
GROUPS = 4
SUB = 8
SUBW = 16
CENT = 256
EFF = 768
TOP = 8
ROWS = 128
CTX_DEV = 1024
LEN = 32768
EXPERTS = 128
CAP = 16
N_CTX = 32


def shared_book(key, salt):
    values = jax.random.normal(jax.random.fold_in(key, salt), (GROUPS, SUB, CENT, SUBW), jnp.float32)
    return jnp.clip(values, -4.0, 4.0)


def draw_key_book(key, part):
    return shared_book(key, 101).astype(jnp.bfloat16)


def draw_queries(key, part):
    width = SUB * SUBW
    base = jnp.clip(jax.random.normal(jax.random.fold_in(key, 7), (ROWS, GROUPS, QH, width), jnp.float32), -5.0, 5.0)
    row_scale = jnp.exp(jax.random.uniform(jax.random.fold_in(key, 8), (ROWS, 1, 1, 1), jnp.float32, math.log(0.5), math.log(2.0)))
    entries = base * row_scale
    result = entries
    return result.reshape(ROWS, GROUPS, QH * width).astype(jnp.bfloat16)


def draw_key_codes(key, part):
    code_values = jax.random.randint(jax.random.fold_in(key, 3), (GROUPS, ROWS, SUB, LEN), 0, CENT, jnp.int32)
    positions = jnp.arange(LEN, dtype=jnp.int32)[None, None, None, :]
    sub_ids = jnp.arange(SUB, dtype=jnp.int32)[None, None, :, None]
    code_values = jnp.where(positions % 64 == 5, 0, code_values)
    code_values = jnp.where(positions % 64 == 9, jnp.where(sub_ids == 0, 1, 0), code_values)
    return code_values.astype(jnp.int32)


def draw_lengths(key, part):
    drawn = jax.random.randint(jax.random.fold_in(key, 5), (ROWS,), 1, LEN + 1, jnp.int32)
    longest = jax.random.randint(jax.random.fold_in(key, 6), (), 0, ROWS, jnp.int32)
    return jnp.where(jnp.arange(ROWS, dtype=jnp.int32) == longest, LEN, drawn).astype(jnp.int32)


def draw_resid(key, part):
    columns = jnp.arange(D, dtype=jnp.float32)[None, :] / D
    col_scale = 3.0 ** columns * jnp.exp(jax.random.uniform(jax.random.fold_in(key, 12), (1, D), jnp.float32, -0.4, 0.4))
    row_scale = jnp.exp(jax.random.uniform(jax.random.fold_in(key, 13), (ROWS, 1), jnp.float32, math.log(0.3), math.log(3.0)))
    base = jnp.clip(jax.random.normal(jax.random.fold_in(key, 14), (ROWS, D), jnp.float32), -5.0, 5.0)
    return (base * col_scale * row_scale).astype(jnp.bfloat16)


def place_ends(values, own_key, low, largest):
    index_at = [jax.random.randint(jax.random.fold_in(own_key, axis), (), 0, length) for axis, length in enumerate(values.shape)]
    main_axis = values.shape.index(max(values.shape))
    beside = index_at[:main_axis] + [(index_at[main_axis] + 1) % values.shape[main_axis]] + index_at[main_axis + 1:]
    return values.at[tuple(index_at)].set(low).at[tuple(beside)].set(largest)


def block_scale(key, shape, shards, least, top_value):
    gain, own = 1.0, jax.random.fold_in(key, 6)
    for axis_at, blocks in shards:
        draws = jnp.exp(jax.random.uniform(jax.random.fold_in(own, axis_at), (blocks,), jnp.float32, least / len(shards), top_value / len(shards)))
        gain = gain * jnp.repeat(draws, shape[axis_at] // blocks).reshape([-1 if axis == axis_at else 1 for axis in range(len(shape))])
    return gain


def deal_out(stream_key, own, number, rows, count, top, most, skew):
    ranking = jax.random.permutation(stream_key, count)
    crowded, ordinary = portions_of(count, rows * top, most, skew, True), portions_of(count, rows * top, most, skew, False)
    places = jnp.arange(count)

    def named(sizes, rotation):
        used = int((sizes > 0).sum())
        fixed = max(1, used // 4)
        passed = fixed + (places - fixed + rotation * (used - fixed)) % max(1, count - fixed)
        return jnp.zeros((count,), jnp.int32).at[ranking[jnp.where(places < fixed, places, passed)]].set(jnp.asarray(sizes, jnp.int32))

    sizes = jnp.where(number % 4 == 0, named(crowded, number // 4), named(ordinary, number - number // 4 - 1))
    mixed = jax.random.permutation(jax.random.fold_in(own, 3), count)
    source_of, receiver = mixed[0:count // 2 * 2:2], mixed[1:count // 2 * 2:2]
    margin = jnp.minimum(sizes[source_of] - 1, most - sizes[receiver]) // 2
    margin = jnp.where((source_of == ranking[0]) | (receiver == ranking[0]) | (sizes[receiver] == 0), 0, jnp.maximum(margin, 0))
    passed = jax.random.randint(jax.random.fold_in(own, 4), (count // 2,), 0, 1 << 20) % (margin + 1)
    sizes = sizes.at[source_of].add(-passed).at[receiver].add(passed)
    labels = jnp.searchsorted(jnp.cumsum(sizes), jnp.arange(rows * top), side="right").astype(jnp.int32)
    grid = labels.reshape(top, rows).T
    grid = grid[jax.random.permutation(jax.random.fold_in(own, 1), rows)]
    rotation = jax.random.randint(jax.random.fold_in(own, 2), (rows, 1), 0, top)
    return jnp.take_along_axis(grid, (jnp.arange(top)[None, :] + rotation) % top, axis=1)


def portions_of(number_of, total, limit, slope, full):
    portions = [(1 << 20) // math.isqrt(standing ** slope) + 1 for standing in range(1, number_of + 1)]
    largest = limit if full else min(limit, max(-(-total // number_of), total * portions[0] // sum(portions)))
    least = 1 if total - largest >= number_of - 1 else 0
    holding, rest = [largest] + [least] * (number_of - 1), total - largest - least * (number_of - 1)
    while rest > 0:
        free = [i for i in range(1, number_of) if holding[i] < largest] or [i for i in range(1, number_of) if holding[i] < limit]
        mass, budget = sum([portions[i] for i in free]), rest
        for i in free:
            addition = min(limit - holding[i], max(1, budget * portions[i] // mass), rest)
            holding[i] = holding[i] + addition
            rest = rest - addition
    return np.array(holding)


def scatter_about(stream_key, extent, scale, bound, cuts=(), kind=jnp.bfloat16):
    values = scale * jax.random.normal(stream_key, extent, jnp.float32)
    if cuts:
        values = values * block_scale(stream_key, extent, cuts, -0.22, 0.18)
    return jnp.clip(values, -bound, bound).astype(kind)


def setup_inputs(seed: int = 0) -> dict:
    streams_of = jax.random.split(jax.random.key(seed), 15)
    queries = draw_queries(jax.random.fold_in(streams_of[14], 71), 0)
    key_codes = draw_key_codes(jax.random.fold_in(streams_of[14], 71), 0)
    value_codes = place_ends(jax.random.randint(streams_of[2], (GROUPS, ROWS, SUB, LEN), 0, CENT), jax.random.fold_in(streams_of[2], 1), 0, CENT - 1).astype(jnp.int32)
    key_book = draw_key_book(jax.random.fold_in(streams_of[14], 71), 0)
    value_book = scatter_about(streams_of[4], (GROUPS, SUB, CENT, SUBW), 1.0, 4.0, ((0, 4),))
    lengths = draw_lengths(jax.random.fold_in(streams_of[14], 71), 0)
    resid = draw_resid(jax.random.fold_in(streams_of[14], 71), 0)
    w_out = scatter_about(streams_of[7], (GROUPS, QH * SUB * SUBW, D), (16 / (GROUPS * QH * SUB * SUBW) ** 0.5), 2.5, ((0, 4), (2, 32)))
    norm_gain = jnp.clip(1.0 + 0.15 * jax.random.normal(streams_of[8], (D,), jnp.float32), 0.25, 1.75).astype(jnp.bfloat16)
    routes_keys = jax.random.split(jax.random.fold_in(streams_of[9], 1), ROWS // ROWS)
    routes_turns = jax.random.permutation(jax.random.fold_in(streams_of[9], 3), ROWS // ROWS)
    routes = jax.vmap(lambda own, number: deal_out(jax.random.fold_in(streams_of[9], 2), own, number, ROWS, EXPERTS, TOP, CAP, 2))(routes_keys, routes_turns).reshape((ROWS, TOP))
    route_weights = jnp.clip(jnp.exp(jax.random.uniform(streams_of[10], (ROWS, TOP), jnp.float32, math.log(0.1), math.log(1.0))), 0.1, 1.0)
    w_gate = scatter_about(streams_of[11], (EXPERTS, D, EFF), D ** -0.5, 0.09375, ((0, 128),))
    w_up = scatter_about(streams_of[12], (EXPERTS, D, EFF), D ** -0.5, 0.09375, ((0, 128),))
    w_down = scatter_about(streams_of[13], (EXPERTS, EFF, D), EFF ** -0.5, 0.21875, ((0, 128),))
    return dict(queries=queries, key_codes=key_codes, value_codes=value_codes, key_book=key_book, value_book=value_book, lengths=lengths, resid=resid, w_out=w_out, norm_gain=norm_gain, routes=routes, route_weights=route_weights, w_gate=w_gate, w_up=w_up, w_down=w_down)


masked_score = -1e+30
epsilon = 1e-06

def dequantize(codebook, code_values):
    subs = jnp.arange(codebook.shape[0], dtype=jnp.int32)[:, None]
    picked = codebook[subs, code_values]
    return jnp.transpose(picked, (1, 0, 2)).reshape(code_values.shape[1], -1)

def one_row(query_row, key_row, value_row, row_length, key_table, value_table):
    key_vectors = dequantize(key_table, key_row)
    value_vectors = dequantize(value_table, value_row)
    head_size = key_vectors.shape[1]
    heads = query_row.reshape(QH, head_size)
    scores = jnp.dot(heads, key_vectors.T, preferred_element_type=jnp.float32) * (1.0 / math.sqrt(head_size))
    scores = scores.reshape(QH, N_CTX, CTX_DEV)
    positions = jnp.arange(LEN, dtype=jnp.int32).reshape(N_CTX, CTX_DEV)
    visible = positions[None, :, :] < row_length
    maxima = lax.optimization_barrier(jnp.max(jnp.where(visible, scores, masked_score), axis=-1))
    weights = jnp.exp(jnp.where(visible, scores - maxima[..., None], masked_score))
    totals = lax.optimization_barrier(jnp.sum(weights, axis=-1))
    weights16 = weights.astype(jnp.bfloat16).astype(jnp.float32)
    slices = value_vectors.reshape(N_CTX, CTX_DEV, head_size).astype(jnp.float32)
    partial_out = jnp.einsum('hnt,ntd->hnd', weights16, slices)
    highest = lax.optimization_barrier(jnp.max(maxima, axis=1))
    factors = jnp.exp(maxima - highest[:, None])
    summed_total = lax.optimization_barrier(jnp.sum(totals * factors, axis=1))
    summed_out = lax.optimization_barrier(jnp.sum(partial_out * factors[..., None], axis=1))
    return (summed_out / summed_total[:, None]).astype(jnp.bfloat16).reshape(-1)

def reference(queries, key_codes, value_codes, key_book, value_book, lengths, resid, w_out, norm_gain, routes, route_weights, w_gate, w_up, w_down):

    def group_attention(packed):
        query_group, key_group, value_group, key_table, value_table = packed

        def row_attention(row_pack):
            return one_row(row_pack[0], row_pack[1], row_pack[2], row_pack[3], key_table, value_table)
        return lax.map(row_attention, (query_group, key_group, value_group, lengths))
    attended = lax.map(group_attention, (jnp.transpose(queries, (1, 0, 2)), key_codes, value_codes, key_book, value_book))
    attended = jnp.transpose(attended, (1, 0, 2)).reshape(ROWS, -1)
    projected = jnp.dot(attended, w_out.reshape(-1, D), preferred_element_type=jnp.float32)
    residual = (resid.astype(jnp.float32) + projected).astype(jnp.bfloat16)
    whole = residual.astype(jnp.float32)
    normed = (whole * lax.rsqrt(lax.optimization_barrier(jnp.mean(whole * whole, axis=1)) + epsilon)[:, None] * norm_gain.astype(jnp.float32)).astype(jnp.bfloat16)

    def expert_step(running, packed):
        expert_id, gate_matrix, up_matrix, down_matrix = packed
        chosen = routes == expert_id
        routed = jnp.any(chosen, axis=1)
        weight_col = lax.optimization_barrier(jnp.sum(jnp.where(chosen, route_weights, 0.0), axis=1))
        slot_index = jnp.cumsum(routed.astype(jnp.int32)) - 1
        slots = jnp.arange(CAP, dtype=jnp.int32)[:, None]
        selector = ((slot_index[None, :] == slots) & routed[None, :]).astype(jnp.float32)
        taken_rows = jnp.dot(selector, normed.astype(jnp.float32), precision=lax.Precision.HIGHEST).astype(jnp.bfloat16)
        gate_act = jnp.dot(taken_rows, gate_matrix, preferred_element_type=jnp.float32)
        up_act = jnp.dot(taken_rows, up_matrix, preferred_element_type=jnp.float32)
        hidden = (jax.nn.silu(gate_act) * up_act).astype(jnp.bfloat16)
        expert_out = jnp.dot(hidden, down_matrix, preferred_element_type=jnp.float32).astype(jnp.bfloat16)
        spread = jnp.dot(selector.T, expert_out.astype(jnp.float32), precision=lax.Precision.HIGHEST)
        return (running + spread * weight_col[:, None], None)
    expert_ids = jnp.arange(EXPERTS, dtype=jnp.int32)
    mixture, unused = lax.scan(expert_step, jnp.zeros((ROWS, D), jnp.float32), (expert_ids, w_gate, w_up, w_down))
    return (residual.astype(jnp.float32) + mixture).astype(jnp.bfloat16)
```

```python
import functools, math
import jax, jax.numpy as jnp
from jax import lax
from jax.experimental import pallas as pl
from jax.experimental.pallas import tpu as pltpu
from jax.sharding import PartitionSpec as P
LOG2E = 1.4426950408889634
f32, bf16, i32 = jnp.float32, jnp.bfloat16, jnp.int32
ROWS, CH, CAP, N_CTX, N_HEAD = 128, 16, 16, 32, 4
MESH = pl.DeviceIdType.MESH

def pow2_scale(x):
    sc = jnp.ones_like(x)
    for p in (32, 16, 8, 4, 2, 1):
        f = float(2.0 ** p)
        ok = x * f <= 4.0
        x = jnp.where(ok, x * f, x)
        sc = jnp.where(ok, sc * f, sc)
    return sc

def build_table(book_ref, table_ref):
    top = jnp.zeros((8, 256), f32)
    for d in range(16):
        top = jnp.maximum(top, jnp.abs(book_ref[d].astype(f32)))
    sc = pow2_scale(jnp.max(top, axis=1, keepdims=True))
    for p in range(8):
        hi = jnp.round(book_ref[2 * p].astype(f32) * (sc * 4096.0)).astype(i32)
        lo = jnp.round(book_ref[2 * p + 1].astype(f32) * (sc * 4096.0)).astype(i32)
        word = hi * 65536 + lo
        table_ref[2 * p] = word[:, :128]
        table_ref[2 * p + 1] = word[:, 128:]
    inv = 1.0 / sc * (2.0 ** -28)
    lane = lax.broadcasted_iota(i32, (8, 128), 1)
    sub = lax.broadcasted_iota(i32, (8, 128), 0)
    return jnp.sum(jnp.where(lane % 8 == sub, inv, 0.0), axis=0, keepdims=True)

def attn_kernel(len_ref, q_ref, kb_ref, vb_ref, gain_ref, kc_hbm, vc_hbm,
                o_ref, kc_ref, vc_ref, kt_ref, vt_ref, qp_ref, ox_ref, key_ref, val_ref, ml_ref, ksem, vsem, *, unroll, SL):
    def code_copy(c, hbm, vmem, sem):
        at = pl.ds(c * CH, CH)
        return pltpu.make_async_copy(hbm.at[0, at], vmem.at[at], sem.at[c])
    for c in range(ROWS // CH):
        code_copy(c, kc_hbm, kc_ref, ksem).start()
        code_copy(c, vc_hbm, vc_ref, vsem).start()
    offset = lax.axis_index("ctx") * 1024
    k_inv = build_table(kb_ref, kt_ref)
    v_inv = build_table(vb_ref, vt_ref)
    i = lax.broadcasted_iota(i32, (128, 128), 0)
    j = lax.broadcasted_iota(i32, (128, 128), 1)
    to_ds = (i // 16 == j % 8) & (i % 16 == j // 8)
    to_sd = (j // 16 == i % 8) & (j % 16 == i // 8)
    qp_ref[...] = jnp.dot(q_ref[...], jnp.where(to_ds, k_inv, 0.0).astype(bf16), preferred_element_type=f32).astype(bf16)
    ml_ref[...] = jnp.zeros_like(ml_ref)
    lane = lax.broadcasted_iota(i32, (16, 128), 1)
    pos = lax.broadcasted_iota(i32, (16, 1024), 1)
    C = 1.0 / math.sqrt(128.0)

    def dequant(codes_ref, b, table_ref, dst_ref, slot):
        for j in range(8):
            at = slice(j * 128, (j + 1) * 128)
            idx = codes_ref[b, :, at]
            low = idx & 127
            upper = idx > 127
            for p in range(8):
                w0 = jnp.take_along_axis(table_ref[2 * p], low, axis=1, mode="promise_in_bounds")
                w1 = jnp.take_along_axis(table_ref[2 * p + 1], low, axis=1, mode="promise_in_bounds")
                w = jnp.where(upper, w1, w0)
                pair = jnp.concatenate([w.astype(f32), (w << 16).astype(f32)], axis=0)
                dst_ref[slot, p * 16:(p + 1) * 16, at] = pair.astype(bf16)

    def fetch(b, slot):
        dequant(kc_ref, b, kt_ref, key_ref, slot)
        dequant(vc_ref, b, vt_ref, val_ref, slot)

    def row(b, slot):
        at = pl.ds(pl.multiple_of(b * 16, 16), 16)
        raw = jnp.dot(qp_ref[at, :], key_ref[slot], preferred_element_type=f32)
        vis = pos < len_ref[b] - offset
        raw = jnp.where(vis, raw, -1e30)
        top = jnp.max(raw, axis=1, keepdims=True)
        w = jnp.where(vis, jnp.exp2((raw - top) * (C * LOG2E)), 0.0)
        tot = jnp.sum(w, axis=1, keepdims=True)
        out = lax.dot_general(w.astype(bf16), val_ref[slot], (((1,), (1,)), ((), ())), preferred_element_type=f32)
        ox_ref[at, :] = (out * v_inv).astype(bf16)
        here = lane == b
        ml_ref[0] = jnp.where(here, top * C, ml_ref[0])
        ml_ref[1] = jnp.where(here, tot, ml_ref[1])

    def wait_chunk(c):
        code_copy(c, kc_hbm, kc_ref, ksem).wait()
        code_copy(c, vc_hbm, vc_ref, vsem).wait()
    wait_chunk(0)
    fetch(0, 0)

    def chunk(c, _):
        @pl.when(c < ROWS // CH - 1)
        def _():
            wait_chunk(c + 1)
        def body(i, _):
            b = c * CH + i * unroll
            for u in range(unroll):
                fetch(jnp.minimum(b + u + 1, ROWS - 1), (u + 1) % SL)
                row(b + u, u % SL)
            return 0
        lax.fori_loop(0, CH // unroll, body, 0)
        return 0
    lax.fori_loop(0, ROWS // CH, chunk, 0)
    r = lax.broadcasted_iota(i32, (256, 256), 0)
    c = lax.broadcasted_iota(i32, (256, 256), 1)
    swap = ((r // 16 == c % 16) & (r % 16 == c // 16)).astype(f32).astype(bf16)
    perm = jnp.where(to_sd, 1.0, 0.0).astype(bf16)
    for g in range(8):
        y = jnp.dot(swap, ox_ref[g * 256:(g + 1) * 256], preferred_element_type=f32).astype(bf16)
        y = jnp.dot(y, perm, preferred_element_type=f32).astype(bf16)
        for h in range(16):
            o_ref[h * 2 + g // 4, g % 4 * 16:g % 4 * 16 + 16, :] = y[h * 16:(h + 1) * 16]

    def three(x):
        hi = x.astype(bf16).astype(f32)
        mid = (x - hi).astype(bf16).astype(f32)
        return hi, mid, x - hi - mid
    pieces = three(ml_ref[0]) + three(ml_ref[1])
    line = lax.broadcasted_iota(i32, (16, 128), 0)
    gain = jnp.where(line == 6, gain_ref[...].astype(f32), 0.0)
    for h in range(16):
        tail = gain
        for k in range(6):
            tail = jnp.where(line == k, pieces[k][h:h + 1, :], tail)
        o_ref[2 * h, 64:80, :] = tail.astype(bf16)
        o_ref[2 * h + 1, 64:80, :] = tail.astype(bf16)

def attend(queries, key_codes, value_codes, key_book, value_book, lengths, norm_gain, unroll=4, SL=2):
    vm = pl.BlockSpec(memory_space=pltpu.VMEM)
    hbm = pl.BlockSpec(memory_space=pl.ANY)
    return pl.pallas_call(
        functools.partial(attn_kernel, unroll=unroll, SL=SL),
        in_specs=[pl.BlockSpec(memory_space=pltpu.SMEM), vm, vm, vm, vm, hbm, hbm],
        out_specs=vm,
        out_shape=jax.ShapeDtypeStruct((N_CTX, 80, 128), bf16),
        scratch_shapes=[pltpu.VMEM((ROWS, 8, 1024), i32), pltpu.VMEM((ROWS, 8, 1024), i32),
                        pltpu.VMEM((16, 8, 128), i32), pltpu.VMEM((16, 8, 128), i32),
                        pltpu.VMEM((2048, 128), bf16), pltpu.VMEM((2048, 128), bf16),
                        pltpu.VMEM((SL, 128, 1024), bf16), pltpu.VMEM((SL, 128, 1024), bf16),
                        pltpu.VMEM((2, 16, 128), f32),
                        pltpu.SemaphoreType.DMA((8,)), pltpu.SemaphoreType.DMA((8,))],
        compiler_params=pltpu.CompilerParams(vmem_limit_bytes=56 << 20),
    )(lengths, queries.reshape(2048, 128), jnp.transpose(key_book[0], (2, 0, 1)),
      jnp.transpose(value_book[0], (2, 0, 1)), norm_gain.reshape(1, 128), key_codes, value_codes)


def rest_kernel(msg_ref, resid_ref, wout_hbm, routes_ref, rw_ref, wg_hbm, wu_hbm, wd_hbm,
                out_ref,
                wout_ref, wg_ref, wu_ref, wd_ref, got_ref, att_ref, zsum_ref, take_ref, taken_ref, xn_ref,
                eo_ref, eogot_ref, part_ref, partgot_ref, gt_ref, sel_ref, selw_ref, wt_ref, res_ref,
                load_sem, send_sem, recv_sem):
    ctx = lax.axis_index("ctx")
    head = lax.axis_index("head")
    loads = [pltpu.make_async_copy(wout_hbm.at[0], wout_ref, load_sem.at[0]),
             pltpu.make_async_copy(wg_hbm.at[0], wg_ref, load_sem.at[1]),
             pltpu.make_async_copy(wu_hbm.at[0], wu_ref, load_sem.at[2]),
             pltpu.make_async_copy(wd_hbm.at[0], wd_ref, load_sem.at[3])]
    barrier = pltpu.get_barrier_semaphore()

    def greet_ctx(k, _):
        pl.semaphore_signal(barrier, inc=1, device_id={"ctx": lax.rem(ctx + k, N_CTX)}, device_id_type=MESH)
        return 0
    lax.fori_loop(1, N_CTX, greet_ctx, 0)
    for k in range(1, N_HEAD):
        pl.semaphore_signal(barrier, inc=1, device_id={"head": lax.rem(head + k, N_HEAD)}, device_id_type=MESH)
    pl.semaphore_wait(barrier, N_CTX - 1 + N_HEAD - 1)

    def send_all(phase, source, target):
        def step(k, _):
            to = lax.rem(ctx + k, N_CTX)
            pltpu.make_async_remote_copy(
                src_ref=source(to), dst_ref=target, send_sem=send_sem.at[phase], recv_sem=recv_sem.at[phase],
                device_id={"ctx": to}, device_id_type=MESH).start()
            return 0
        lax.fori_loop(1, N_CTX, step, 0)

    def wait_all(sems, phase, ref, count):
        view = ref.at[pl.ds(0, count)]
        pltpu.make_async_copy(view, view, sems.at[phase]).wait()

    send_all(0, lambda to: msg_ref.at[to], got_ref.at[ctx])
    for load in loads:
        load.start()
    got_ref[ctx] = msg_ref[ctx]

    eye = (lax.broadcasted_iota(i32, (8, 8), 0) == lax.broadcasted_iota(i32, (8, 8), 1)).astype(f32).astype(bf16)
    flip = lambda x: lax.dot_general(eye, x, (((1,), (1,)), ((), ())), preferred_element_type=f32)
    names = flip(routes_ref[...].astype(f32).astype(bf16)).astype(i32)
    rw = rw_ref[...]
    rw_hi = rw.astype(bf16)
    rw_mid = (rw - rw_hi.astype(f32)).astype(bf16)
    rw_lo = (rw - rw_hi.astype(f32) - rw_mid.astype(f32)).astype(bf16)
    shares = flip(rw_hi) + flip(rw_mid) + flip(rw_lo)
    expert = lax.broadcasted_iota(i32, (N_CTX, ROWS), 0) * N_HEAD + head
    member = jnp.zeros((N_CTX, ROWS), f32)
    weight = jnp.zeros((N_CTX, ROWS), f32)
    for k in range(8):
        same = names[k:k + 1, :] == expert
        member = jnp.where(same, 1.0, member)
        weight = jnp.where(same, shares[k:k + 1, :], weight)
    before = (lax.broadcasted_iota(i32, (ROWS, ROWS), 0) < lax.broadcasted_iota(i32, (ROWS, ROWS), 1)).astype(f32).astype(bf16)
    slot = jnp.dot(member.astype(bf16), before, preferred_element_type=f32).astype(i32)
    slot = jnp.where(member > 0.5, slot, -1)
    slots = lax.broadcasted_iota(i32, (CAP, ROWS), 0)
    for e in range(N_CTX):
        hit = slot[e:e + 1, :] == slots
        sel_ref[e * CAP:(e + 1) * CAP, :] = jnp.where(hit, 1.0, 0.0).astype(bf16)
        selw_ref[e * CAP:(e + 1) * CAP, :] = jnp.where(hit, weight[e:e + 1, :], 0.0)
    for t in range(N_CTX * CAP // 128):
        block = selw_ref[t * 128:(t + 1) * 128, :].T
        hi = block.astype(bf16)
        rest = block - hi.astype(f32)
        mid = rest.astype(bf16)
        wt_ref[0, :, t * 128:(t + 1) * 128] = hi
        wt_ref[1, :, t * 128:(t + 1) * 128] = mid
        wt_ref[2, :, t * 128:(t + 1) * 128] = (rest - mid.astype(f32)).astype(bf16)

    wait_all(recv_sem, 0, got_ref, N_CTX - 1)
    tails = got_ref[:, 64:80, :].reshape(N_CTX * 16, 128)
    r = lax.broadcasted_iota(i32, (3 * N_CTX, N_CTX * 16), 0)
    c = lax.broadcasted_iota(i32, (3 * N_CTX, N_CTX * 16), 1)
    kind, at = r // N_CTX, c % 16
    wanted = (c // 16 == r % N_CTX) & (at // 3 == kind) & (at < 7)
    stats = jnp.dot(jnp.where(wanted, 1.0, 0.0).astype(bf16), tails, preferred_element_type=f32)
    maxima, totals, gain = stats[:N_CTX], stats[N_CTX:2 * N_CTX], stats[2 * N_CTX:]
    factor = jnp.exp(maxima - jnp.max(maxima, axis=0, keepdims=True))
    factor = factor / jnp.sum(factor * totals, axis=0, keepdims=True)
    gt_ref[...] = jnp.concatenate([factor, jnp.zeros((ROWS - N_CTX, ROWS), f32)], axis=0).T
    mine = gt_ref[pl.ds(pl.multiple_of(lax.rem(ctx, 2) * 64, 64), 64), :]
    total = jnp.zeros((64, 128), f32)
    for s in range(N_CTX):
        total += mine[:, s:s + 1] * got_ref[s, :64, :].astype(f32)
    att_ref[ctx] = total.astype(bf16)
    send_all(1, lambda to: att_ref.at[ctx], att_ref.at[ctx])
    loads[0].wait()
    wait_all(recv_sem, 1, att_ref, N_CTX - 1)
    proj = jnp.zeros((ROWS, 128), f32)
    for h in range(16):
        rows = att_ref[2 * h:2 * h + 2].reshape(ROWS, 128)
        proj += jnp.dot(rows, wout_ref[h * 128:(h + 1) * 128, :], preferred_element_type=f32)

    def send_heads(phase, source, target):
        for k in range(1, N_HEAD):
            to = lax.rem(head + k, N_HEAD)
            pltpu.make_async_remote_copy(
                src_ref=source(to), dst_ref=target, send_sem=send_sem.at[phase], recv_sem=recv_sem.at[phase],
                device_id={"head": to}, device_id_type=MESH).start()

    zsum_ref[head] = proj
    send_heads(2, lambda to: zsum_ref.at[head], zsum_ref.at[head])
    wait_all(recv_sem, 2, zsum_ref, N_HEAD - 1)
    projected = (zsum_ref[0] + zsum_ref[1]) + (zsum_ref[2] + zsum_ref[3])
    residual = (resid_ref[...].astype(f32) + projected).astype(bf16)
    res_ref[...] = residual.astype(f32)

    take_ref[...] = jnp.dot(sel_ref[...], residual, preferred_element_type=f32).astype(bf16).reshape(N_CTX, CAP, 128)
    send_all(3, lambda to: take_ref.at[to], taken_ref.at[ctx])
    taken_ref[ctx] = take_ref[ctx]
    loads[1].wait()
    loads[2].wait()
    loads[3].wait()
    wait_all(recv_sem, 3, taken_ref, N_CTX - 1)
    squares = jnp.zeros((CAP, 128), f32)
    for s in range(N_CTX):
        piece = taken_ref[s].astype(f32)
        squares += piece * piece
    scale = lax.rsqrt(jnp.sum(squares, axis=1, keepdims=True) * (1.0 / 4096) + 1e-6)
    for s in range(N_CTX):
        piece = taken_ref[s].astype(f32) * scale * gain[s:s + 1, :]
        xn_ref[s // 4, :, s % 4 * 128:s % 4 * 128 + 128] = piece.astype(bf16)

    def up_step(k, acc):
        rows = pl.ds(pl.multiple_of(k * 512, 512), 512)
        x = xn_ref[k]
        return (acc[0] + jnp.dot(x, wg_ref[rows, :], preferred_element_type=f32),
                acc[1] + jnp.dot(x, wu_ref[rows, :], preferred_element_type=f32))
    zero = jnp.zeros((CAP, 768), f32)
    gate, up = lax.fori_loop(0, 8, up_step, (zero, zero))
    hidden = (gate / (1.0 + jnp.exp(-gate)) * up).astype(bf16)

    def down_step(n, _):
        y = jnp.dot(hidden, wd_ref[:, pl.ds(pl.multiple_of(n * 512, 512), 512)], preferred_element_type=f32).astype(bf16)
        for q in range(4):
            eo_ref[n * 4 + q] = y[:, q * 128:(q + 1) * 128]
        return 0
    lax.fori_loop(0, 8, down_step, 0)
    send_all(4, lambda to: eo_ref.at[to], eogot_ref.at[ctx])
    eogot_ref[ctx] = eo_ref[ctx]
    wait_all(recv_sem, 4, eogot_ref, N_CTX - 1)
    outs = eogot_ref[...].reshape(N_CTX * CAP, 128)
    part = jnp.dot(wt_ref[0], outs, preferred_element_type=f32)
    part += jnp.dot(wt_ref[1], outs, preferred_element_type=f32) + jnp.dot(wt_ref[2], outs, preferred_element_type=f32)
    part_ref[...] = part.reshape(N_HEAD, 32, 128)
    send_heads(5, lambda to: part_ref.at[to], partgot_ref.at[head])
    partgot_ref[head] = part_ref[head]
    wait_all(recv_sem, 5, partgot_ref, N_HEAD - 1)
    mixture = (partgot_ref[0] + partgot_ref[1]) + (partgot_ref[2] + partgot_ref[3])
    own = res_ref[pl.ds(pl.multiple_of(head * 32, 32), 32), :]
    out_ref[...] = (own + mixture).astype(bf16)
    wait_all(send_sem, 0, msg_ref, N_CTX - 1)
    wait_all(send_sem, 1, att_ref, N_CTX - 1)
    wait_all(send_sem, 2, zsum_ref, N_HEAD - 1)
    wait_all(send_sem, 3, take_ref, N_CTX - 1)
    wait_all(send_sem, 4, eo_ref, N_CTX - 1)
    wait_all(send_sem, 5, part_ref, N_HEAD - 1)


def rest(message, resid, w_out, routes, route_weights, w_gate, w_up, w_down):
    vm = pl.BlockSpec(memory_space=pltpu.VMEM)
    hbm = pl.BlockSpec(memory_space=pl.ANY)
    V = pltpu.VMEM
    return pl.pallas_call(
        rest_kernel,
        in_specs=[vm, vm, hbm, vm, vm, hbm, hbm, hbm],
        out_specs=vm,
        out_shape=jax.ShapeDtypeStruct((32, 128), bf16),
        scratch_shapes=[
            V((2048, 128), bf16), V((4096, 768), bf16), V((4096, 768), bf16), V((768, 4096), bf16),
            V((N_CTX, 80, 128), bf16), V((N_CTX, 64, 128), bf16), V((N_HEAD, ROWS, 128), f32),
            V((N_CTX, CAP, 128), bf16), V((N_CTX, CAP, 128), bf16), V((8, CAP, 512), bf16),
            V((N_CTX, CAP, 128), bf16), V((N_CTX, CAP, 128), bf16), V((N_HEAD, 32, 128), f32), V((N_HEAD, 32, 128), f32),
            V((ROWS, ROWS), f32), V((N_CTX * CAP, 128), bf16), V((N_CTX * CAP, 128), f32), V((3, ROWS, N_CTX * CAP), bf16),
            V((ROWS, 128), f32),
            pltpu.SemaphoreType.DMA((4,)), pltpu.SemaphoreType.DMA((6,)), pltpu.SemaphoreType.DMA((6,)),
        ],
        compiler_params=pltpu.CompilerParams(vmem_limit_bytes=48 << 20, collective_id=0, has_side_effects=True),
    )(message, resid, w_out, routes, route_weights, w_gate, w_up, w_down)


def on_device(queries, key_codes, value_codes, key_book, value_book, lengths, resid, w_out, norm_gain,
              routes, route_weights, w_gate, w_up, w_down):
    message = attend(queries, key_codes, value_codes, key_book, value_book, lengths, norm_gain)
    return rest(message, resid, w_out, routes, route_weights, w_gate, w_up, w_down)


def solution(mesh):
    return jax.shard_map(
        on_device,
        mesh=mesh,
        in_specs=(
            P(None, "head", None),
            P("head", None, None, "ctx"),
            P("head", None, None, "ctx"),
            P("head", None, None, None),
            P("head", None, None, None),
            P(),
            P(None, "ctx"),
            P("head", None, "ctx"),
            P("ctx"),
            P(),
            P(),
            P(("ctx", "head"), None, None),
            P(("ctx", "head"), None, None),
            P(("ctx", "head"), None, None),
        ),
        out_specs=P("head", "ctx"),
        check_vma=False,
    )
```

```python
import functools, math
import jax, jax.numpy as jnp
from jax import lax
from jax.experimental import pallas as pl
from jax.experimental.pallas import tpu as pltpu
from jax.sharding import PartitionSpec as P
LOG2E = 1.4426950408889634
f32, bf16, i32 = jnp.float32, jnp.bfloat16, jnp.int32
ROWS, CH, CAP, N_CTX, N_HEAD = 128, 16, 16, 32, 4
UNROLL, SLOTS, AHEAD = 8, 4, 2
MESH = pl.DeviceIdType.MESH

def pow2_scale(x):
    sc = jnp.ones_like(x)
    for p in (32, 16, 8, 4, 2, 1):
        f = float(2.0 ** p)
        ok = x * f <= 4.0
        x = jnp.where(ok, x * f, x)
        sc = jnp.where(ok, sc * f, sc)
    return sc

def build_table(book_ref, table_ref):
    top = jnp.zeros((8, 256), f32)
    for d in range(16):
        top = jnp.maximum(top, jnp.abs(book_ref[d].astype(f32)))
    sc = pow2_scale(jnp.max(top, axis=1, keepdims=True))
    for p in range(8):
        hi = jnp.round(book_ref[2 * p].astype(f32) * (sc * 4096.0)).astype(i32)
        lo = jnp.round(book_ref[2 * p + 1].astype(f32) * (sc * 4096.0)).astype(i32)
        word = hi * 65536 + lo
        table_ref[2 * p] = word[:, :128]
        table_ref[2 * p + 1] = word[:, 128:]
    inv = 1.0 / sc * (2.0 ** -28)
    lane = lax.broadcasted_iota(i32, (8, 128), 1)
    sub = lax.broadcasted_iota(i32, (8, 128), 0)
    return jnp.sum(jnp.where(lane % 8 == sub, inv, 0.0), axis=0, keepdims=True)

def layer_kernel(len_ref, q_ref, kb_ref, vb_ref, gain_ref, resid_ref, routes_ref, rw_ref,
                 kc_hbm, vc_hbm, wout_hbm, wg_hbm, wu_hbm, wd_hbm,
                 out_ref,
                 kc_ref, vc_ref, kt_ref, vt_ref, qp_ref, ox_ref, key_ref, val_ref, ml_ref, swap_ref, msg_ref,
                 wout_ref, wg_ref, wu_ref, wd_ref, got_ref, att_ref, zsum_ref, take_ref, taken_ref, xn_ref,
                 eo_ref, eogot_ref, part_ref, partgot_ref, gt_ref, sel_ref, selw_ref, wt_ref, res_ref,
                 ksem, vsem, load_sem, send_sem, recv_sem):
    ctx = lax.axis_index("ctx")
    head = lax.axis_index("head")
    core = lax.rem(ctx, 2)
    chip = ctx // 2
    barrier = pltpu.get_barrier_semaphore()

    def greet_ctx(k, _):
        pl.semaphore_signal(barrier, inc=1, device_id={"ctx": lax.rem(ctx + k, N_CTX)}, device_id_type=MESH)
        return 0
    lax.fori_loop(1, N_CTX, greet_ctx, 0)
    for k in range(1, N_HEAD):
        pl.semaphore_signal(barrier, inc=1, device_id={"head": lax.rem(head + k, N_HEAD)}, device_id_type=MESH)

    def code_copy(c, hbm, vmem, sem):
        at = pl.ds(c * CH, CH)
        return pltpu.make_async_copy(hbm.at[0, at], vmem.at[at], sem.at[c])
    for c in range(ROWS // CH):
        code_copy(c, kc_hbm, kc_ref, ksem).start()
        code_copy(c, vc_hbm, vc_ref, vsem).start()
    loads = [pltpu.make_async_copy(wout_hbm.at[0], wout_ref, load_sem.at[0]),
             pltpu.make_async_copy(wg_hbm.at[0], wg_ref, load_sem.at[1]),
             pltpu.make_async_copy(wu_hbm.at[0], wu_ref, load_sem.at[2]),
             pltpu.make_async_copy(wd_hbm.at[0], wd_ref, load_sem.at[3])]
    for load in loads:
        load.start()

    offset = ctx * 1024
    k_inv = build_table(kb_ref, kt_ref)
    v_inv = build_table(vb_ref, vt_ref)
    i = lax.broadcasted_iota(i32, (128, 128), 0)
    j = lax.broadcasted_iota(i32, (128, 128), 1)
    to_ds = (i // 16 == j % 8) & (i % 16 == j // 8)
    to_sd = (j // 16 == i % 8) & (j % 16 == i // 8)
    perm = jnp.where(to_sd, 1.0, 0.0).astype(bf16)
    qp_ref[...] = jnp.dot(q_ref[...], jnp.where(to_ds, k_inv, 0.0).astype(bf16), preferred_element_type=f32).astype(bf16)
    ml_ref[...] = jnp.zeros_like(ml_ref)
    ox_ref[...] = jnp.zeros_like(ox_ref)
    r = lax.broadcasted_iota(i32, (256, 256), 0)
    c = lax.broadcasted_iota(i32, (256, 256), 1)
    swap_ref[...] = ((r // 16 == c % 16) & (r % 16 == c // 16)).astype(f32).astype(bf16)
    lane = lax.broadcasted_iota(i32, (16, 128), 1)
    pos = lax.broadcasted_iota(i32, (16, 1024), 1)
    C = 1.0 / math.sqrt(128.0)

    def three(x):
        hi = x.astype(bf16)
        rest = x - hi.astype(f32)
        mid = rest.astype(bf16)
        return hi, mid, (rest - mid.astype(f32)).astype(bf16)

    def dequant(codes_ref, b, table_ref, dst_ref, slot):
        for j in range(8):
            at = slice(j * 128, (j + 1) * 128)
            idx = codes_ref[b, :, at]
            low = idx & 127
            upper = idx > 127
            for p in range(8):
                w0 = jnp.take_along_axis(table_ref[2 * p], low, axis=1, mode="promise_in_bounds")
                w1 = jnp.take_along_axis(table_ref[2 * p + 1], low, axis=1, mode="promise_in_bounds")
                w = jnp.where(upper, w1, w0)
                pair = jnp.concatenate([w.astype(f32), (w << 16).astype(f32)], axis=0)
                dst_ref[slot, p * 16:(p + 1) * 16, at] = pair.astype(bf16)

    def fetch(b, slot):
        dequant(kc_ref, b, kt_ref, key_ref, slot)
        dequant(vc_ref, b, vt_ref, val_ref, slot)

    def row(b, slot):
        at = pl.ds(pl.multiple_of(b * 16, 16), 16)
        raw = jnp.dot(qp_ref[at, :], key_ref[slot], preferred_element_type=f32)
        vis = pos < len_ref[b] - offset
        raw = jnp.where(vis, raw, -1e30)
        top = raw[:, 0:128]
        for k in range(1, 8):
            top = jnp.maximum(top, raw[:, k * 128:(k + 1) * 128])
        top = jnp.max(top, axis=1, keepdims=True)
        w = jnp.where(vis, jnp.exp2((raw - top) * (C * LOG2E)), 0.0)
        tot = w[:, 0:128]
        for k in range(1, 8):
            tot = tot + w[:, k * 128:(k + 1) * 128]
        tot = jnp.dot(jnp.concatenate(three(tot), axis=1), jnp.ones((384, 128), bf16), preferred_element_type=f32)
        out = lax.dot_general(w.astype(bf16), val_ref[slot], (((1,), (1,)), ((), ())), preferred_element_type=f32)
        ox_ref[at, :] = (out * v_inv).astype(bf16)
        here = lane == b
        ml_ref[0] = jnp.where(here, top * C, ml_ref[0])
        ml_ref[1] = jnp.where(here, tot, ml_ref[1])

    def turn(c, part):
        y = jnp.dot(swap_ref[pl.ds(pl.multiple_of(part * 128, 128), 128), :],
                    ox_ref[pl.ds(pl.multiple_of(c * 256, 256), 256), :], preferred_element_type=f32).astype(bf16)
        y = jnp.dot(y, perm, preferred_element_type=f32).astype(bf16)
        at = pl.ds(pl.multiple_of(lax.rem(c, 4) * 16, 16), 16)
        for h in range(8):
            msg_ref[(part * 8 + h) * 2 + c // 4, at, :] = y[h * 16:(h + 1) * 16]

    def add_tail(half):
        pieces = [x.astype(f32) for x in three(ml_ref[0]) + three(ml_ref[1])]
        line = lax.broadcasted_iota(i32, (16, 128), 0)
        gain = jnp.where(line == 6, gain_ref[...].astype(f32), 0.0)
        for h in range(16):
            tail = gain
            for k in range(6):
                tail = jnp.where(line == k, pieces[k][h:h + 1, :], tail)
            msg_ref[2 * h + half, 64:80, :] = tail.astype(bf16)

    def remote(phase, src, dst, to):
        return pltpu.make_async_remote_copy(
            src_ref=src, dst_ref=dst, send_sem=send_sem.at[phase], recv_sem=recv_sem.at[phase],
            device_id=to, device_id_type=MESH)

    def send_quarter(q):
        half = q // 2
        rows = pl.ds(0, 32) if q % 2 == 0 else pl.ds(32, 48)

        def step(k, _):
            to = lax.rem(chip + k, 16) * 2 + half
            @pl.when(to != ctx)
            def _():
                remote(0, msg_ref.at[to, rows], got_ref.at[ctx, rows], {"ctx": to}).start()
            return 0
        lax.fori_loop(0, 16, step, 0)

    def send_all(phase, source, target):
        def step(k, _):
            to = lax.rem(ctx + k, N_CTX)
            remote(phase, source(to), target, {"ctx": to}).start()
            return 0
        lax.fori_loop(1, N_CTX, step, 0)

    def wait_all(sems, phase, ref, count):
        view = ref.at[pl.ds(0, count)]
        pltpu.make_async_copy(view, view, sems.at[phase]).wait()

    def send_heads(phase, source, target):
        for k in range(1, N_HEAD):
            to = lax.rem(head + k, N_HEAD)
            remote(phase, source(to), target, {"head": to}).start()

    def wait_chunk(c):
        code_copy(c, kc_hbm, kc_ref, ksem).wait()
        code_copy(c, vc_hbm, vc_ref, vsem).wait()
    wait_chunk(0)
    for b in range(AHEAD):
        fetch(b, b)
    pl.semaphore_wait(barrier, N_CTX - 1 + N_HEAD - 1)

    def chunk(c, _):
        @pl.when(c < ROWS // CH - 1)
        def _():
            wait_chunk(c + 1)

        def body(i, _):
            b = c * CH + i * UNROLL
            turn(jnp.maximum(c - 1, 0), i)
            for u in range(UNROLL):
                fetch(jnp.minimum(b + u + AHEAD, ROWS - 1), (u + AHEAD) % SLOTS)
                row(b + u, u % SLOTS)
            return 0
        lax.fori_loop(0, CH // UNROLL, body, 0)
        for q in range(3):
            @pl.when(c == 2 * q + 2)
            def _():
                if q == 1:
                    add_tail(0)
                send_quarter(q)
        return 0
    lax.fori_loop(0, ROWS // CH, chunk, 0)
    turn(ROWS // CH - 1, 0)
    turn(ROWS // CH - 1, 1)
    add_tail(1)
    send_quarter(3)
    got_ref[ctx] = msg_ref[ctx]

    eye = (lax.broadcasted_iota(i32, (8, 8), 0) == lax.broadcasted_iota(i32, (8, 8), 1)).astype(f32).astype(bf16)
    flip = lambda x: lax.dot_general(eye, x, (((1,), (1,)), ((), ())), preferred_element_type=f32)
    names = flip(routes_ref[...].astype(f32).astype(bf16)).astype(i32)
    rw = rw_ref[...]
    rw_hi = rw.astype(bf16)
    rw_mid = (rw - rw_hi.astype(f32)).astype(bf16)
    rw_lo = (rw - rw_hi.astype(f32) - rw_mid.astype(f32)).astype(bf16)
    shares = flip(rw_hi) + flip(rw_mid) + flip(rw_lo)
    expert = lax.broadcasted_iota(i32, (N_CTX, ROWS), 0) * N_HEAD + head
    member = jnp.zeros((N_CTX, ROWS), f32)
    weight = jnp.zeros((N_CTX, ROWS), f32)
    for k in range(8):
        same = names[k:k + 1, :] == expert
        member = jnp.where(same, 1.0, member)
        weight = jnp.where(same, shares[k:k + 1, :], weight)
    before = (lax.broadcasted_iota(i32, (ROWS, ROWS), 0) < lax.broadcasted_iota(i32, (ROWS, ROWS), 1)).astype(f32).astype(bf16)
    slot = jnp.dot(member.astype(bf16), before, preferred_element_type=f32).astype(i32)
    slot = jnp.where(member > 0.5, slot, -1)
    slots = lax.broadcasted_iota(i32, (CAP, ROWS), 0)
    for e in range(N_CTX):
        hit = slot[e:e + 1, :] == slots
        sel_ref[e * CAP:(e + 1) * CAP, :] = jnp.where(hit, 1.0, 0.0).astype(bf16)
        selw_ref[e * CAP:(e + 1) * CAP, :] = jnp.where(hit, weight[e:e + 1, :], 0.0)
    for t in range(N_CTX * CAP // 128):
        block = selw_ref[t * 128:(t + 1) * 128, :].T
        hi = block.astype(bf16)
        rest = block - hi.astype(f32)
        mid = rest.astype(bf16)
        wt_ref[0, :, t * 128:(t + 1) * 128] = hi
        wt_ref[1, :, t * 128:(t + 1) * 128] = mid
        wt_ref[2, :, t * 128:(t + 1) * 128] = (rest - mid.astype(f32)).astype(bf16)

    wait_all(recv_sem, 0, got_ref, N_CTX - 1)
    tails = got_ref[:, 64:80, :].reshape(N_CTX * 16, 128)
    r = lax.broadcasted_iota(i32, (3 * N_CTX, N_CTX * 16), 0)
    c = lax.broadcasted_iota(i32, (3 * N_CTX, N_CTX * 16), 1)
    kind, at = r // N_CTX, c % 16
    wanted = (c // 16 == r % N_CTX) & (at // 3 == kind) & (at < 7)
    stats = jnp.dot(jnp.where(wanted, 1.0, 0.0).astype(bf16), tails, preferred_element_type=f32)
    maxima, totals, gain = stats[:N_CTX], stats[N_CTX:2 * N_CTX], stats[2 * N_CTX:]
    factor = jnp.exp(maxima - jnp.max(maxima, axis=0, keepdims=True))
    factor = factor / jnp.sum(factor * totals, axis=0, keepdims=True)
    gt_ref[...] = jnp.concatenate([factor, jnp.zeros((ROWS - N_CTX, ROWS), f32)], axis=0).T
    mine = gt_ref[pl.ds(pl.multiple_of(core * 64, 64), 64), :]
    total = jnp.zeros((64, 128), f32)
    for s in range(N_CTX):
        total += mine[:, s:s + 1] * got_ref[s, :64, :].astype(f32)
    att_ref[core, chip] = total.astype(bf16)
    mine = att_ref.at[core, chip]

    def share(k, _):
        remote(1, mine, mine, {"ctx": lax.rem(chip + k, 16) * 2 + core}).start()
        return 0
    lax.fori_loop(1, 16, share, 0)
    loads[0].wait()
    wait_all(recv_sem, 1, att_ref.at[core], 15)
    sibling = remote(2, att_ref.at[core], att_ref.at[core], {"ctx": ctx + 1 - 2 * core})
    sibling.start()

    def project(half):
        proj = jnp.zeros((64, 128), f32)
        for h in range(16):
            proj += jnp.dot(att_ref[half, h], wout_ref[h * 128:(h + 1) * 128, :], preferred_element_type=f32)
        zsum_ref[head, half] = proj
        send_heads(3, lambda to: zsum_ref.at[head, half], zsum_ref.at[head, half])
    project(core)
    sibling.wait()
    project(1 - core)
    wait_all(recv_sem, 3, zsum_ref, N_HEAD - 1)
    projected = (zsum_ref[0] + zsum_ref[1]) + (zsum_ref[2] + zsum_ref[3])
    residual = (resid_ref[...].astype(f32) + projected.reshape(ROWS, 128)).astype(bf16)
    res_ref[...] = residual.astype(f32)

    take_ref[...] = jnp.dot(sel_ref[...], residual, preferred_element_type=f32).astype(bf16).reshape(N_CTX, CAP, 128)
    send_all(4, lambda to: take_ref.at[to], taken_ref.at[ctx])
    taken_ref[ctx] = take_ref[ctx]
    loads[1].wait()
    loads[2].wait()
    loads[3].wait()
    wait_all(recv_sem, 4, taken_ref, N_CTX - 1)
    squares = jnp.zeros((CAP, 128), f32)
    for s in range(N_CTX):
        piece = taken_ref[s].astype(f32)
        squares += piece * piece
    scale = lax.rsqrt(jnp.sum(squares, axis=1, keepdims=True) * (1.0 / 4096) + 1e-6)
    for s in range(N_CTX):
        piece = taken_ref[s].astype(f32) * scale * gain[s:s + 1, :]
        xn_ref[s // 4, :, s % 4 * 128:s % 4 * 128 + 128] = piece.astype(bf16)

    def up_step(k, acc):
        rows = pl.ds(pl.multiple_of(k * 512, 512), 512)
        x = xn_ref[k]
        return (acc[0] + jnp.dot(x, wg_ref[rows, :], preferred_element_type=f32),
                acc[1] + jnp.dot(x, wu_ref[rows, :], preferred_element_type=f32))
    zero = jnp.zeros((CAP, 768), f32)
    gate, up = lax.fori_loop(0, 8, up_step, (zero, zero))
    hidden = (gate / (1.0 + jnp.exp(-gate)) * up).astype(bf16)

    def down_step(n, _):
        y = jnp.dot(hidden, wd_ref[:, pl.ds(pl.multiple_of(n * 512, 512), 512)], preferred_element_type=f32).astype(bf16)
        for q in range(4):
            eo_ref[n * 4 + q] = y[:, q * 128:(q + 1) * 128]
        return 0
    lax.fori_loop(0, 8, down_step, 0)
    send_all(5, lambda to: eo_ref.at[to], eogot_ref.at[ctx])
    eogot_ref[ctx] = eo_ref[ctx]
    wait_all(recv_sem, 5, eogot_ref, N_CTX - 1)
    outs = eogot_ref[...].reshape(N_CTX * CAP, 128)
    part = jnp.dot(wt_ref[0], outs, preferred_element_type=f32)
    part += jnp.dot(wt_ref[1], outs, preferred_element_type=f32) + jnp.dot(wt_ref[2], outs, preferred_element_type=f32)
    part_ref[...] = part.reshape(N_HEAD, 32, 128)
    send_heads(6, lambda to: part_ref.at[to], partgot_ref.at[head])
    partgot_ref[head] = part_ref[head]
    wait_all(recv_sem, 6, partgot_ref, N_HEAD - 1)
    mixture = (partgot_ref[0] + partgot_ref[1]) + (partgot_ref[2] + partgot_ref[3])
    own = res_ref[pl.ds(pl.multiple_of(head * 32, 32), 32), :]
    out_ref[...] = (own + mixture).astype(bf16)
    wait_all(send_sem, 0, msg_ref, N_CTX - 1)
    wait_all(send_sem, 1, att_ref.at[core], 15)
    wait_all(send_sem, 3, zsum_ref, N_HEAD - 1)
    wait_all(send_sem, 4, take_ref, N_CTX - 1)
    wait_all(send_sem, 5, eo_ref, N_CTX - 1)
    wait_all(send_sem, 6, part_ref, N_HEAD - 1)


def on_device(queries, key_codes, value_codes, key_book, value_book, lengths, resid, w_out, norm_gain,
              routes, route_weights, w_gate, w_up, w_down):
    vm = pl.BlockSpec(memory_space=pltpu.VMEM)
    hbm = pl.BlockSpec(memory_space=pl.ANY)
    V = pltpu.VMEM
    dma = pltpu.SemaphoreType.DMA
    return pl.pallas_call(
        layer_kernel,
        in_specs=[pl.BlockSpec(memory_space=pltpu.SMEM)] + [vm] * 7 + [hbm] * 6,
        out_specs=vm,
        out_shape=jax.ShapeDtypeStruct((32, 128), bf16),
        scratch_shapes=[
            V((ROWS, 8, 1024), i32), V((ROWS, 8, 1024), i32), V((16, 8, 128), i32), V((16, 8, 128), i32),
            V((2048, 128), bf16), V((2048, 128), bf16), V((SLOTS, 128, 1024), bf16), V((SLOTS, 128, 1024), bf16),
            V((2, 16, 128), f32), V((256, 256), bf16), V((N_CTX, 80, 128), bf16),
            V((2048, 128), bf16), V((4096, 768), bf16), V((4096, 768), bf16), V((768, 4096), bf16),
            V((N_CTX, 80, 128), bf16), V((2, 16, 64, 128), bf16), V((N_HEAD, 2, 64, 128), f32),
            V((N_CTX, CAP, 128), bf16), V((N_CTX, CAP, 128), bf16), V((8, CAP, 512), bf16),
            V((N_CTX, CAP, 128), bf16), V((N_CTX, CAP, 128), bf16), V((N_HEAD, 32, 128), f32), V((N_HEAD, 32, 128), f32),
            V((ROWS, ROWS), f32), V((N_CTX * CAP, 128), bf16), V((N_CTX * CAP, 128), f32), V((3, ROWS, N_CTX * CAP), bf16),
            V((ROWS, 128), f32),
            dma((8,)), dma((8,)), dma((4,)), dma((7,)), dma((7,)),
        ],
        compiler_params=pltpu.CompilerParams(vmem_limit_bytes=58 << 20, collective_id=0, has_side_effects=True),
    )(lengths, queries.reshape(2048, 128), jnp.transpose(key_book[0], (2, 0, 1)),
      jnp.transpose(value_book[0], (2, 0, 1)), norm_gain.reshape(1, 128), resid, routes, route_weights,
      key_codes, value_codes, w_out, w_gate, w_up, w_down)


def solution(mesh):
    return jax.shard_map(
        on_device,
        mesh=mesh,
        in_specs=(
            P(None, "head", None),
            P("head", None, None, "ctx"),
            P("head", None, None, "ctx"),
            P("head", None, None, None),
            P("head", None, None, None),
            P(),
            P(None, "ctx"),
            P("head", None, "ctx"),
            P("ctx"),
            P(),
            P(),
            P(("ctx", "head"), None, None),
            P(("ctx", "head"), None, None),
            P(("ctx", "head"), None, None),
        ),
        out_specs=P("head", "ctx"),
        check_vma=False,
    )
```

```python
import functools, math
import jax, jax.numpy as jnp
from jax import lax
from jax.experimental import pallas as pl
from jax.experimental.pallas import tpu as pltpu
from jax.sharding import PartitionSpec as P
LOG2E = 1.4426950408889634
f32, bf16, i32 = jnp.float32, jnp.bfloat16, jnp.int32
ROWS, CH, CAP, N_CTX, N_HEAD = 128, 16, 16, 32, 4
UNROLL, SLOTS, AHEAD = 8, 4, 2
MESH = pl.DeviceIdType.MESH

def pow2_scale(x):
    sc = jnp.ones_like(x)
    for p in (32, 16, 8, 4, 2, 1):
        f = float(2.0 ** p)
        ok = x * f <= 4.0
        x = jnp.where(ok, x * f, x)
        sc = jnp.where(ok, sc * f, sc)
    return sc

def build_table(book_ref, table_ref, turn):
    rows = jnp.dot(turn, book_ref[...].reshape(128, 256), preferred_element_type=f32)
    entries = [rows[8 * d:8 * d + 8] for d in range(16)]
    top = jnp.abs(entries[0])
    for d in range(1, 16):
        top = jnp.maximum(top, jnp.abs(entries[d]))
    sc = pow2_scale(jnp.max(top, axis=1, keepdims=True))
    for p in range(8):
        hi = jnp.round(entries[2 * p] * (sc * 4096.0)).astype(i32)
        lo = jnp.round(entries[2 * p + 1] * (sc * 4096.0)).astype(i32)
        word = hi * 65536 + lo
        table_ref[2 * p] = word[:, :128]
        table_ref[2 * p + 1] = word[:, 128:]
    inv = 1.0 / sc * (2.0 ** -28)
    lane = lax.broadcasted_iota(i32, (8, 128), 1)
    sub = lax.broadcasted_iota(i32, (8, 128), 0)
    return jnp.sum(jnp.where(lane % 8 == sub, inv, 0.0), axis=0, keepdims=True)

def layer_kernel(len_ref, q_ref, kb_ref, vb_ref, gain_ref, resid_ref, routes_ref, rw_ref,
                 kc_hbm, vc_hbm, wout_hbm, wg_hbm, wu_hbm, wd_hbm,
                 out_ref,
                 kc_ref, vc_ref, kt_ref, vt_ref, qp_ref, ox_ref, key_ref, val_ref, ml_ref, swap_ref, msg_ref,
                 wout_ref, wg_ref, wu_ref, wd_ref, got_ref, att_ref, zsum_ref, take_ref, taken_ref, xn_ref,
                 eo_ref, eogot_ref, part_ref, partgot_ref, gt_ref, sel_ref, selw_ref, wt_ref, res_ref,
                 ksem, vsem, load_sem, send_sem, recv_sem):
    ctx = lax.axis_index("ctx")
    head = lax.axis_index("head")
    core = lax.rem(ctx, 2)
    chip = ctx // 2
    barrier = pltpu.get_barrier_semaphore()

    def greet_ctx(k, _):
        pl.semaphore_signal(barrier, inc=1, device_id={"ctx": lax.rem(ctx + k, N_CTX)}, device_id_type=MESH)
        return 0
    lax.fori_loop(1, N_CTX, greet_ctx, 0)
    for k in range(1, N_HEAD):
        pl.semaphore_signal(barrier, inc=1, device_id={"head": lax.rem(head + k, N_HEAD)}, device_id_type=MESH)

    def code_copy(c, hbm, vmem, sem):
        at = pl.ds(c * CH, CH)
        return pltpu.make_async_copy(hbm.at[0, at], vmem.at[at], sem.at[c])
    for c in range(ROWS // CH):
        code_copy(c, kc_hbm, kc_ref, ksem).start()
        code_copy(c, vc_hbm, vc_ref, vsem).start()
    loads = [pltpu.make_async_copy(wout_hbm.at[0], wout_ref, load_sem.at[0]),
             pltpu.make_async_copy(wg_hbm.at[0], wg_ref, load_sem.at[1]),
             pltpu.make_async_copy(wu_hbm.at[0], wu_ref, load_sem.at[2]),
             pltpu.make_async_copy(wd_hbm.at[0], wd_ref, load_sem.at[3])]
    for load in loads:
        load.start()

    offset = ctx * 1024
    i = lax.broadcasted_iota(i32, (128, 128), 0)
    j = lax.broadcasted_iota(i32, (128, 128), 1)
    to_ds = (i // 16 == j % 8) & (i % 16 == j // 8)
    to_sd = (j // 16 == i % 8) & (j % 16 == i // 8)
    perm = jnp.where(to_sd, 1.0, 0.0).astype(bf16)
    k_inv = build_table(kb_ref, kt_ref, perm)
    v_inv = build_table(vb_ref, vt_ref, perm)
    ml_ref[...] = jnp.zeros_like(ml_ref)
    ox_ref[...] = jnp.zeros_like(ox_ref)
    r = lax.broadcasted_iota(i32, (256, 256), 0)
    c = lax.broadcasted_iota(i32, (256, 256), 1)
    swap_ref[...] = ((r // 16 == c % 16) & (r % 16 == c // 16)).astype(f32).astype(bf16)
    k_perm = jnp.where(to_ds, k_inv, 0.0).astype(bf16)
    for g in range(ROWS // CH):
        x = jnp.concatenate([q_ref[g * CH:(g + 1) * CH, h * 128:(h + 1) * 128] for h in range(16)], axis=0)
        x = jnp.dot(swap_ref[...], x, preferred_element_type=f32).astype(bf16)
        qp_ref[g * 256:(g + 1) * 256, :] = jnp.dot(x, k_perm, preferred_element_type=f32).astype(bf16)
    lane = lax.broadcasted_iota(i32, (16, 128), 1)
    pos = lax.broadcasted_iota(i32, (16, 1024), 1)
    C = 1.0 / math.sqrt(128.0)

    def three(x):
        hi = x.astype(bf16)
        rest = x - hi.astype(f32)
        mid = rest.astype(bf16)
        return hi, mid, (rest - mid.astype(f32)).astype(bf16)

    def dequant(codes_ref, b, table_ref, dst_ref, slot):
        for j in range(8):
            at = slice(j * 128, (j + 1) * 128)
            idx = codes_ref[b, :, at]
            low = idx & 127
            upper = idx > 127
            for p in range(8):
                w0 = jnp.take_along_axis(table_ref[2 * p], low, axis=1, mode="promise_in_bounds")
                w1 = jnp.take_along_axis(table_ref[2 * p + 1], low, axis=1, mode="promise_in_bounds")
                w = jnp.where(upper, w1, w0)
                pair = jnp.concatenate([w.astype(f32), (w << 16).astype(f32)], axis=0)
                dst_ref[slot, p * 16:(p + 1) * 16, at] = pair.astype(bf16)

    def fetch(b, slot):
        dequant(kc_ref, b, kt_ref, key_ref, slot)
        dequant(vc_ref, b, vt_ref, val_ref, slot)

    def row(b, slot):
        at = pl.ds(pl.multiple_of(b * 16, 16), 16)
        raw = jnp.dot(qp_ref[at, :], key_ref[slot], preferred_element_type=f32)
        vis = pos < len_ref[b] - offset
        raw = jnp.where(vis, raw, -1e30)
        top = raw[:, 0:128]
        for k in range(1, 8):
            top = jnp.maximum(top, raw[:, k * 128:(k + 1) * 128])
        top = jnp.max(top, axis=1, keepdims=True)
        w = jnp.where(vis, jnp.exp2((raw - top) * (C * LOG2E)), 0.0)
        tot = w[:, 0:128]
        for k in range(1, 8):
            tot = tot + w[:, k * 128:(k + 1) * 128]
        tot = jnp.dot(jnp.concatenate(three(tot), axis=1), jnp.ones((384, 128), bf16), preferred_element_type=f32)
        out = lax.dot_general(w.astype(bf16), val_ref[slot], (((1,), (1,)), ((), ())), preferred_element_type=f32)
        ox_ref[at, :] = (out * v_inv).astype(bf16)
        here = lane == b
        ml_ref[0] = jnp.where(here, top * C, ml_ref[0])
        ml_ref[1] = jnp.where(here, tot, ml_ref[1])

    def turn(c, part):
        y = jnp.dot(swap_ref[pl.ds(pl.multiple_of(part * 128, 128), 128), :],
                    ox_ref[pl.ds(pl.multiple_of(c * 256, 256), 256), :], preferred_element_type=f32).astype(bf16)
        y = jnp.dot(y, perm, preferred_element_type=f32).astype(bf16)
        at = pl.ds(pl.multiple_of(lax.rem(c, 4) * 16, 16), 16)
        for h in range(8):
            msg_ref[(part * 8 + h) * 2 + c // 4, at, :] = y[h * 16:(h + 1) * 16]

    def add_tail(half):
        pieces = [x.astype(f32) for x in three(ml_ref[0]) + three(ml_ref[1])]
        line = lax.broadcasted_iota(i32, (16, 128), 0)
        gain = jnp.where(line == 6, gain_ref[...].astype(f32), 0.0)
        for h in range(16):
            tail = gain
            for k in range(6):
                tail = jnp.where(line == k, pieces[k][h:h + 1, :], tail)
            msg_ref[2 * h + half, 64:80, :] = tail.astype(bf16)

    def remote(phase, src, dst, to):
        return pltpu.make_async_remote_copy(
            src_ref=src, dst_ref=dst, send_sem=send_sem.at[phase], recv_sem=recv_sem.at[phase],
            device_id=to, device_id_type=MESH)

    def send_quarter(q):
        half = q // 2
        rows = pl.ds(0, 32) if q % 2 == 0 else pl.ds(32, 48)

        for k in range(1, 16):
            to = lax.rem(chip + k, 16) * 2 + half
            remote(0, msg_ref.at[to, rows], got_ref.at[ctx, rows], {"ctx": to}).start()

        @pl.when(core != half)
        def _():
            to = chip * 2 + half
            remote(0, msg_ref.at[to, rows], got_ref.at[ctx, rows], {"ctx": to}).start()

    def send_all(phase, source, target):
        for k in range(1, N_CTX):
            to = lax.rem(ctx + k, N_CTX)
            remote(phase, source(to), target, {"ctx": to}).start()

    def wait_all(sems, phase, ref, count):
        view = ref.at[pl.ds(0, count)]
        pltpu.make_async_copy(view, view, sems.at[phase]).wait()

    def send_heads(phase, source, target):
        for k in range(1, N_HEAD):
            to = lax.rem(head + k, N_HEAD)
            remote(phase, source(to), target, {"head": to}).start()

    def wait_chunk(c):
        code_copy(c, kc_hbm, kc_ref, ksem).wait()
        code_copy(c, vc_hbm, vc_ref, vsem).wait()
    wait_chunk(0)
    for b in range(AHEAD):
        fetch(b, b)
    pl.semaphore_wait(barrier, N_CTX - 1 + N_HEAD - 1)

    def chunk(c, _):
        @pl.when(c < ROWS // CH - 1)
        def _():
            wait_chunk(c + 1)

        def body(i, _):
            b = c * CH + i * UNROLL
            turn(jnp.maximum(c - 1, 0), i)
            for u in range(UNROLL):
                fetch(jnp.minimum(b + u + AHEAD, ROWS - 1), (u + AHEAD) % SLOTS)
                row(b + u, u % SLOTS)
            return 0
        lax.fori_loop(0, CH // UNROLL, body, 0)
        for q in range(3):
            @pl.when(c == 2 * q + 2)
            def _():
                if q == 1:
                    add_tail(0)
                send_quarter(q)
        return 0
    lax.fori_loop(0, ROWS // CH, chunk, 0)
    turn(ROWS // CH - 1, 0)
    turn(ROWS // CH - 1, 1)
    add_tail(1)
    send_quarter(3)
    got_ref[ctx] = msg_ref[ctx]

    names, shares = routes_ref[...], rw_ref[...]
    expert = lax.broadcasted_iota(i32, (N_CTX, ROWS), 0) * N_HEAD + head
    member = jnp.zeros((N_CTX, ROWS), f32)
    weight = jnp.zeros((N_CTX, ROWS), f32)
    for k in range(8):
        same = names[k:k + 1, :] == expert
        member = jnp.where(same, 1.0, member)
        weight = jnp.where(same, shares[k:k + 1, :], weight)
    before = (lax.broadcasted_iota(i32, (ROWS, ROWS), 0) < lax.broadcasted_iota(i32, (ROWS, ROWS), 1)).astype(f32).astype(bf16)
    slot = jnp.dot(member.astype(bf16), before, preferred_element_type=f32).astype(i32)
    slot = jnp.where(member > 0.5, slot, -1)
    slots = lax.broadcasted_iota(i32, (CAP, ROWS), 0)
    for e in range(N_CTX):
        hit = slot[e:e + 1, :] == slots
        sel_ref[e * CAP:(e + 1) * CAP, :] = jnp.where(hit, 1.0, 0.0).astype(bf16)
        selw_ref[e * CAP:(e + 1) * CAP, :] = jnp.where(hit, weight[e:e + 1, :], 0.0)
    for t in range(N_CTX * CAP // 128):
        block = selw_ref[t * 128:(t + 1) * 128, :].T
        hi = block.astype(bf16)
        rest = block - hi.astype(f32)
        mid = rest.astype(bf16)
        wt_ref[0, :, t * 128:(t + 1) * 128] = hi
        wt_ref[1, :, t * 128:(t + 1) * 128] = mid
        wt_ref[2, :, t * 128:(t + 1) * 128] = (rest - mid.astype(f32)).astype(bf16)

    wait_all(recv_sem, 0, got_ref, N_CTX - 1)
    tails = got_ref[:, 64:80, :].reshape(N_CTX * 16, 128)
    r = lax.broadcasted_iota(i32, (3 * N_CTX, N_CTX * 16), 0)
    c = lax.broadcasted_iota(i32, (3 * N_CTX, N_CTX * 16), 1)
    kind, at = r // N_CTX, c % 16
    wanted = (c // 16 == r % N_CTX) & (at // 3 == kind) & (at < 7)
    stats = jnp.dot(jnp.where(wanted, 1.0, 0.0).astype(bf16), tails, preferred_element_type=f32)
    maxima, totals, gain = stats[:N_CTX], stats[N_CTX:2 * N_CTX], stats[2 * N_CTX:]
    factor = jnp.exp(maxima - jnp.max(maxima, axis=0, keepdims=True))
    factor = factor / jnp.sum(factor * totals, axis=0, keepdims=True)
    gt_ref[...] = jnp.concatenate([factor, jnp.zeros((ROWS - N_CTX, ROWS), f32)], axis=0).T
    mine = gt_ref[pl.ds(pl.multiple_of(core * 64, 64), 64), :]
    total = jnp.zeros((64, 128), f32)
    for s in range(N_CTX):
        total += mine[:, s:s + 1] * got_ref[s, :64, :].astype(f32)
    att_ref[core, chip] = total.astype(bf16)
    mine = att_ref.at[core, chip]

    for k in range(1, 16):
        remote(1, mine, mine, {"ctx": lax.rem(chip + k, 16) * 2 + core}).start()
    loads[0].wait()
    wait_all(recv_sem, 1, att_ref.at[core], 15)
    sibling = remote(2, att_ref.at[core], att_ref.at[core], {"ctx": ctx + 1 - 2 * core})
    sibling.start()

    def project(half):
        proj = jnp.zeros((64, 128), f32)
        for h in range(16):
            proj += jnp.dot(att_ref[half, h], wout_ref[h * 128:(h + 1) * 128, :], preferred_element_type=f32)
        zsum_ref[head, half] = proj.astype(bf16)
        send_heads(3, lambda to: zsum_ref.at[head, half], zsum_ref.at[head, half])
    project(core)
    sibling.wait()
    project(1 - core)
    wait_all(recv_sem, 3, zsum_ref, N_HEAD - 1)
    parts = [zsum_ref[z].astype(f32) for z in range(N_HEAD)]
    projected = (parts[0] + parts[1]) + (parts[2] + parts[3])
    residual = (resid_ref[...].astype(f32) + projected.reshape(ROWS, 128)).astype(bf16)
    res_ref[...] = residual.astype(f32)

    take_ref[...] = jnp.dot(sel_ref[...], residual, preferred_element_type=f32).astype(bf16).reshape(N_CTX, CAP, 128)
    send_all(4, lambda to: take_ref.at[to], taken_ref.at[ctx])
    taken_ref[ctx] = take_ref[ctx]
    loads[1].wait()
    loads[2].wait()
    loads[3].wait()
    wait_all(recv_sem, 4, taken_ref, N_CTX - 1)
    squares = jnp.zeros((CAP, 128), f32)
    for s in range(N_CTX):
        piece = taken_ref[s].astype(f32)
        squares += piece * piece
    scale = lax.rsqrt(jnp.sum(squares, axis=1, keepdims=True) * (1.0 / 4096) + 1e-6)
    for s in range(N_CTX):
        piece = taken_ref[s].astype(f32) * scale * gain[s:s + 1, :]
        xn_ref[s // 4, :, s % 4 * 128:s % 4 * 128 + 128] = piece.astype(bf16)

    def up_step(k, acc):
        rows = pl.ds(pl.multiple_of(k * 512, 512), 512)
        x = xn_ref[k]
        return (acc[0] + jnp.dot(x, wg_ref[rows, :], preferred_element_type=f32),
                acc[1] + jnp.dot(x, wu_ref[rows, :], preferred_element_type=f32))
    zero = jnp.zeros((CAP, 768), f32)
    gate, up = lax.fori_loop(0, 8, up_step, (zero, zero))
    hidden = (gate / (1.0 + jnp.exp(-gate)) * up).astype(bf16)

    def down_step(k, _):
        n = lax.rem(ctx // 4 + k, 8)
        y = jnp.dot(hidden, wd_ref[:, pl.ds(pl.multiple_of(n * 512, 512), 512)], preferred_element_type=f32).astype(bf16)
        for q in range(4):
            to = n * 4 + q
            eo_ref[to] = y[:, q * 128:(q + 1) * 128]

            @pl.when(to != ctx)
            def _():
                remote(5, eo_ref.at[to], eogot_ref.at[ctx], {"ctx": to}).start()
        return 0
    lax.fori_loop(0, 8, down_step, 0)
    eogot_ref[ctx] = eo_ref[ctx]
    wait_all(recv_sem, 5, eogot_ref, N_CTX - 1)
    outs = eogot_ref[...].reshape(N_CTX * CAP, 128)
    part = jnp.dot(wt_ref[0], outs, preferred_element_type=f32)
    part += jnp.dot(wt_ref[1], outs, preferred_element_type=f32) + jnp.dot(wt_ref[2], outs, preferred_element_type=f32)
    part_ref[...] = part.reshape(N_HEAD, 32, 128)
    send_heads(6, lambda to: part_ref.at[to], partgot_ref.at[head])
    partgot_ref[head] = part_ref[head]
    wait_all(recv_sem, 6, partgot_ref, N_HEAD - 1)
    mixture = (partgot_ref[0] + partgot_ref[1]) + (partgot_ref[2] + partgot_ref[3])
    own = res_ref[pl.ds(pl.multiple_of(head * 32, 32), 32), :]
    out_ref[...] = (own + mixture).astype(bf16)
    wait_all(send_sem, 0, msg_ref, N_CTX - 1)
    wait_all(send_sem, 1, att_ref.at[core], 15)
    wait_all(send_sem, 3, zsum_ref, N_HEAD - 1)
    wait_all(send_sem, 4, take_ref, N_CTX - 1)
    wait_all(send_sem, 5, eo_ref, N_CTX - 1)
    wait_all(send_sem, 6, part_ref, N_HEAD - 1)


def on_device(queries, key_codes, value_codes, key_book, value_book, lengths, resid, w_out, norm_gain,
              routes, route_weights, w_gate, w_up, w_down):
    vm = pl.BlockSpec(memory_space=pltpu.VMEM)
    hbm = pl.BlockSpec(memory_space=pl.ANY)
    V = pltpu.VMEM
    dma = pltpu.SemaphoreType.DMA
    return pl.pallas_call(
        layer_kernel,
        in_specs=[pl.BlockSpec(memory_space=pltpu.SMEM)] + [vm] * 7 + [hbm] * 6,
        out_specs=vm,
        out_shape=jax.ShapeDtypeStruct((32, 128), bf16),
        scratch_shapes=[
            V((ROWS, 8, 1024), i32), V((ROWS, 8, 1024), i32), V((16, 8, 128), i32), V((16, 8, 128), i32),
            V((2048, 128), bf16), V((2048, 128), bf16), V((SLOTS, 128, 1024), bf16), V((SLOTS, 128, 1024), bf16),
            V((2, 16, 128), f32), V((256, 256), bf16), V((N_CTX, 80, 128), bf16),
            V((2048, 128), bf16), V((4096, 768), bf16), V((4096, 768), bf16), V((768, 4096), bf16),
            V((N_CTX, 80, 128), bf16), V((2, 16, 64, 128), bf16), V((N_HEAD, 2, 64, 128), bf16),
            V((N_CTX, CAP, 128), bf16), V((N_CTX, CAP, 128), bf16), V((8, CAP, 512), bf16),
            V((N_CTX, CAP, 128), bf16), V((N_CTX, CAP, 128), bf16), V((N_HEAD, 32, 128), f32), V((N_HEAD, 32, 128), f32),
            V((ROWS, ROWS), f32), V((N_CTX * CAP, 128), bf16), V((N_CTX * CAP, 128), f32), V((3, ROWS, N_CTX * CAP), bf16),
            V((ROWS, 128), f32),
            dma((8,)), dma((8,)), dma((4,)), dma((7,)), dma((7,)),
        ],
        compiler_params=pltpu.CompilerParams(vmem_limit_bytes=58 << 20, collective_id=0, has_side_effects=True),
    )(lengths, queries.reshape(ROWS, 2048), jnp.transpose(key_book[0], (0, 2, 1)),
      jnp.transpose(value_book[0], (0, 2, 1)), norm_gain.reshape(1, 128), resid, routes.T, route_weights.T,
      key_codes, value_codes, w_out, w_gate, w_up, w_down)


def solution(mesh):
    return jax.shard_map(
        on_device,
        mesh=mesh,
        in_specs=(
            P(None, "head", None),
            P("head", None, None, "ctx"),
            P("head", None, None, "ctx"),
            P("head", None, None, None),
            P("head", None, None, None),
            P(),
            P(None, "ctx"),
            P("head", None, "ctx"),
            P("ctx"),
            P(),
            P(),
            P(("ctx", "head"), None, None),
            P(("ctx", "head"), None, None),
            P(("ctx", "head"), None, None),
        ),
        out_specs=P("head", "ctx"),
        check_vma=False,
    )
```

```python
import functools, math
import jax, jax.numpy as jnp
from jax import lax
from jax.experimental import pallas as pl
from jax.experimental.pallas import tpu as pltpu
from jax.sharding import PartitionSpec as P
LOG2E = 1.4426950408889634
f32, bf16, i32 = jnp.float32, jnp.bfloat16, jnp.int32
ROWS, CH, CAP, N_CTX, N_HEAD = 128, 16, 16, 32, 4
UNROLL, SLOTS, AHEAD = 16, 4, 2
MESH = pl.DeviceIdType.MESH

def pow2_scale(x):
    sc = jnp.ones_like(x)
    for p in (32, 16, 8, 4, 2, 1):
        f = float(2.0 ** p)
        ok = x * f <= 4.0
        x = jnp.where(ok, x * f, x)
        sc = jnp.where(ok, sc * f, sc)
    return sc

def build_table(book_ref, table_ref, turn):
    rows = jnp.dot(turn, book_ref[...].reshape(128, 256), preferred_element_type=f32)
    entries = [rows[8 * d:8 * d + 8] for d in range(16)]
    top = jnp.abs(entries[0])
    for d in range(1, 16):
        top = jnp.maximum(top, jnp.abs(entries[d]))
    sc = pow2_scale(jnp.max(top, axis=1, keepdims=True))
    for p in range(8):
        hi = jnp.round(entries[2 * p] * (sc * 4096.0)).astype(i32)
        lo = jnp.round(entries[2 * p + 1] * (sc * 4096.0)).astype(i32)
        word = hi * 65536 + lo
        table_ref[2 * p] = word[:, :128]
        table_ref[2 * p + 1] = word[:, 128:]
    inv = 1.0 / sc * (2.0 ** -28)
    lane = lax.broadcasted_iota(i32, (8, 128), 1)
    sub = lax.broadcasted_iota(i32, (8, 128), 0)
    return jnp.sum(jnp.where(lane % 8 == sub, inv, 0.0), axis=0, keepdims=True)

def layer_kernel(len_ref, q_ref, kb_ref, vb_ref, gain_ref, resid_ref, routes_ref, rw_ref,
                 kc_hbm, vc_hbm, wout_hbm, wg_hbm, wu_hbm, wd_hbm,
                 out_ref,
                 kc_ref, vc_ref, kt_ref, vt_ref, qp_ref, ox_ref, key_ref, val_ref, ml_ref, swap_ref, msg_ref,
                 wout_ref, wg_ref, wu_ref, wd_ref, got_ref, att_ref, zsum_ref, take_ref, taken_ref, xn_ref,
                 eo_ref, eogot_ref, part_ref, partgot_ref, gt_ref, sel_ref, selw_ref, wt_ref, res_ref,
                 ksem, vsem, load_sem, send_sem, recv_sem):
    ctx = lax.axis_index("ctx")
    head = lax.axis_index("head")
    core = lax.rem(ctx, 2)
    chip = ctx // 2
    barrier = pltpu.get_barrier_semaphore()

    def greet_ctx(k, _):
        pl.semaphore_signal(barrier, inc=1, device_id={"ctx": lax.rem(ctx + k, N_CTX)}, device_id_type=MESH)
        return 0
    lax.fori_loop(1, N_CTX, greet_ctx, 0)
    for k in range(1, N_HEAD):
        pl.semaphore_signal(barrier, inc=1, device_id={"head": lax.rem(head + k, N_HEAD)}, device_id_type=MESH)

    def code_copy(c, hbm, vmem, sem):
        at = pl.ds(c * CH, CH)
        return pltpu.make_async_copy(hbm.at[0, at], vmem.at[at], sem.at[c])
    for c in range(ROWS // CH):
        code_copy(c, kc_hbm, kc_ref, ksem).start()
        code_copy(c, vc_hbm, vc_ref, vsem).start()
    loads = [pltpu.make_async_copy(wout_hbm.at[0], wout_ref, load_sem.at[0]),
             pltpu.make_async_copy(wg_hbm.at[0], wg_ref, load_sem.at[1]),
             pltpu.make_async_copy(wu_hbm.at[0], wu_ref, load_sem.at[2]),
             pltpu.make_async_copy(wd_hbm.at[0], wd_ref, load_sem.at[3])]
    for load in loads:
        load.start()

    offset = ctx * 1024
    i = lax.broadcasted_iota(i32, (128, 128), 0)
    j = lax.broadcasted_iota(i32, (128, 128), 1)
    to_ds = (i // 16 == j % 8) & (i % 16 == j // 8)
    to_sd = (j // 16 == i % 8) & (j % 16 == i // 8)
    perm = jnp.where(to_sd, 1.0, 0.0).astype(bf16)
    k_inv = build_table(kb_ref, kt_ref, perm)
    v_inv = build_table(vb_ref, vt_ref, perm)
    ml_ref[...] = jnp.zeros_like(ml_ref)
    ox_ref[...] = jnp.zeros_like(ox_ref)
    r = lax.broadcasted_iota(i32, (256, 256), 0)
    c = lax.broadcasted_iota(i32, (256, 256), 1)
    swap_ref[...] = ((r // 16 == c % 16) & (r % 16 == c // 16)).astype(f32).astype(bf16)
    k_perm = jnp.where(to_ds, k_inv, 0.0).astype(bf16)

    def turn_queries(c, part):
        x = q_ref[pl.ds(pl.multiple_of(c * CH, CH), CH), :]
        x = jnp.concatenate([x[:, h * 128:(h + 1) * 128] for h in range(16)], axis=0)
        half = pl.multiple_of(part * 128, 128)
        x = jnp.dot(swap_ref[pl.ds(half, 128), :], x, preferred_element_type=f32).astype(bf16)
        at = pl.ds(pl.multiple_of(c * 256 + half, 128), 128)
        qp_ref[at, :] = jnp.dot(x, k_perm, preferred_element_type=f32).astype(bf16)
    turn_queries(0, 0)
    turn_queries(0, 1)
    lane = lax.broadcasted_iota(i32, (16, 128), 1)
    pos = lax.broadcasted_iota(i32, (16, 1024), 1)
    C = 1.0 / math.sqrt(128.0)

    def three(x):
        hi = x.astype(bf16)
        rest = x - hi.astype(f32)
        mid = rest.astype(bf16)
        return hi, mid, (rest - mid.astype(f32)).astype(bf16)

    def dequant(codes_ref, b, table_ref, dst_ref, slot):
        for j in range(8):
            at = slice(j * 128, (j + 1) * 128)
            idx = codes_ref[b, :, at]
            low = idx & 127
            upper = idx > 127
            for p in range(8):
                w0 = jnp.take_along_axis(table_ref[2 * p], low, axis=1, mode="promise_in_bounds")
                w1 = jnp.take_along_axis(table_ref[2 * p + 1], low, axis=1, mode="promise_in_bounds")
                w = jnp.where(upper, w1, w0)
                pair = jnp.concatenate([w.astype(f32), (w << 16).astype(f32)], axis=0)
                dst_ref[slot, p * 16:(p + 1) * 16, at] = pair.astype(bf16)

    def fetch(b, slot):
        dequant(kc_ref, b, kt_ref, key_ref, slot)
        dequant(vc_ref, b, vt_ref, val_ref, slot)

    def row(b, slot):
        at = pl.ds(pl.multiple_of(b * 16, 16), 16)
        raw = jnp.dot(qp_ref[at, :], key_ref[slot], preferred_element_type=f32)
        vis = pos < len_ref[b] - offset
        raw = jnp.where(vis, raw, -1e30)
        top = raw[:, 0:128]
        for k in range(1, 8):
            top = jnp.maximum(top, raw[:, k * 128:(k + 1) * 128])
        top = jnp.max(top.astype(bf16), axis=1, keepdims=True).astype(f32)
        w = jnp.where(vis, jnp.exp2((raw - top) * (C * LOG2E)), 0.0)
        tot = w[:, 0:128]
        for k in range(1, 8):
            tot = tot + w[:, k * 128:(k + 1) * 128]
        tot = jnp.dot(jnp.concatenate(three(tot), axis=1), jnp.ones((384, 128), bf16), preferred_element_type=f32)
        out = lax.dot_general(w.astype(bf16), val_ref[slot], (((1,), (1,)), ((), ())), preferred_element_type=f32)
        ox_ref[at, :] = (out * v_inv).astype(bf16)
        here = lane == b
        ml_ref[0] = jnp.where(here, top * C, ml_ref[0])
        ml_ref[1] = jnp.where(here, tot, ml_ref[1])

    def turn(c, part):
        y = jnp.dot(swap_ref[pl.ds(pl.multiple_of(part * 128, 128), 128), :],
                    ox_ref[pl.ds(pl.multiple_of(c * 256, 256), 256), :], preferred_element_type=f32).astype(bf16)
        y = jnp.dot(y, perm, preferred_element_type=f32).astype(bf16)
        at = pl.ds(pl.multiple_of(lax.rem(c, 4) * 16, 16), 16)
        for h in range(8):
            msg_ref[(part * 8 + h) * 2 + c // 4, at, :] = y[h * 16:(h + 1) * 16]

    def add_tail(half):
        pieces = [x.astype(f32) for x in three(ml_ref[0]) + three(ml_ref[1])]
        line = lax.broadcasted_iota(i32, (16, 128), 0)
        gain = jnp.where(line == 6, gain_ref[...].astype(f32), 0.0)
        for h in range(16):
            tail = gain
            for k in range(6):
                tail = jnp.where(line == k, pieces[k][h:h + 1, :], tail)
            msg_ref[2 * h + half, 64:80, :] = tail.astype(bf16)

    def remote(phase, src, dst, to):
        return pltpu.make_async_remote_copy(
            src_ref=src, dst_ref=dst, send_sem=send_sem.at[phase], recv_sem=recv_sem.at[phase],
            device_id=to, device_id_type=MESH)

    def send_quarter(q):
        half = q // 2
        rows = pl.ds(0, 32) if q % 2 == 0 else pl.ds(32, 48)

        for k in range(1, 16):
            to = lax.rem(chip + k, 16) * 2 + half
            remote(0, msg_ref.at[to, rows], got_ref.at[ctx, rows], {"ctx": to}).start()

        @pl.when(core != half)
        def _():
            to = chip * 2 + half
            remote(0, msg_ref.at[to, rows], got_ref.at[ctx, rows], {"ctx": to}).start()

    def send_all(phase, source, target):
        for k in range(1, N_CTX):
            to = lax.rem(ctx + k, N_CTX)
            remote(phase, source(to), target, {"ctx": to}).start()

    def wait_all(sems, phase, ref, count):
        view = ref.at[pl.ds(0, count)]
        pltpu.make_async_copy(view, view, sems.at[phase]).wait()

    def send_heads(phase, source, target):
        for k in range(1, N_HEAD):
            to = lax.rem(head + k, N_HEAD)
            remote(phase, source(to), target, {"head": to}).start()

    def wait_chunk(c):
        code_copy(c, kc_hbm, kc_ref, ksem).wait()
        code_copy(c, vc_hbm, vc_ref, vsem).wait()
    wait_chunk(0)
    for b in range(AHEAD):
        fetch(b, b)
    pl.semaphore_wait(barrier, N_CTX - 1 + N_HEAD - 1)

    def chunk(c, _):
        @pl.when(c < ROWS // CH - 1)
        def _():
            wait_chunk(c + 1)

        def body(i, _):
            b = c * CH + i * UNROLL
            for part in range(2) if UNROLL == CH else (i,):
                turn(jnp.maximum(c - 1, 0), part)
                turn_queries(jnp.minimum(c + 1, ROWS // CH - 1), part)
            for u in range(UNROLL):
                fetch(jnp.minimum(b + u + AHEAD, ROWS - 1), (u + AHEAD) % SLOTS)
                row(b + u, u % SLOTS)
            return 0
        lax.fori_loop(0, CH // UNROLL, body, 0)
        for q in range(3):
            @pl.when(c == 2 * q + 2)
            def _():
                if q == 1:
                    add_tail(0)
                send_quarter(q)
        return 0
    lax.fori_loop(0, ROWS // CH, chunk, 0)
    turn(ROWS // CH - 1, 0)
    turn(ROWS // CH - 1, 1)
    add_tail(1)
    send_quarter(3)
    got_ref[ctx] = msg_ref[ctx]

    names, shares = routes_ref[...], rw_ref[...]
    expert = lax.broadcasted_iota(i32, (N_CTX, ROWS), 0) * N_HEAD + head
    member = jnp.zeros((N_CTX, ROWS), f32)
    weight = jnp.zeros((N_CTX, ROWS), f32)
    for k in range(8):
        same = names[k:k + 1, :] == expert
        member = jnp.where(same, 1.0, member)
        weight = jnp.where(same, shares[k:k + 1, :], weight)
    before = (lax.broadcasted_iota(i32, (ROWS, ROWS), 0) < lax.broadcasted_iota(i32, (ROWS, ROWS), 1)).astype(f32).astype(bf16)
    slot = jnp.dot(member.astype(bf16), before, preferred_element_type=f32).astype(i32)
    slot = jnp.where(member > 0.5, slot, -1)
    slots = lax.broadcasted_iota(i32, (CAP, ROWS), 0)
    for e in range(N_CTX):
        hit = slot[e:e + 1, :] == slots
        sel_ref[e * CAP:(e + 1) * CAP, :] = jnp.where(hit, 1.0, 0.0).astype(bf16)
        selw_ref[e * CAP:(e + 1) * CAP, :] = jnp.where(hit, weight[e:e + 1, :], 0.0)
    for t in range(N_CTX * CAP // 128):
        block = selw_ref[t * 128:(t + 1) * 128, :].T
        hi = block.astype(bf16)
        rest = block - hi.astype(f32)
        mid = rest.astype(bf16)
        wt_ref[0, :, t * 128:(t + 1) * 128] = hi
        wt_ref[1, :, t * 128:(t + 1) * 128] = mid
        wt_ref[2, :, t * 128:(t + 1) * 128] = (rest - mid.astype(f32)).astype(bf16)

    wait_all(recv_sem, 0, got_ref, N_CTX - 1)
    tails = got_ref[:, 64:80, :].reshape(N_CTX * 16, 128)
    r = lax.broadcasted_iota(i32, (3 * N_CTX, N_CTX * 16), 0)
    c = lax.broadcasted_iota(i32, (3 * N_CTX, N_CTX * 16), 1)
    kind, at = r // N_CTX, c % 16
    wanted = (c // 16 == r % N_CTX) & (at // 3 == kind) & (at < 7)
    stats = jnp.dot(jnp.where(wanted, 1.0, 0.0).astype(bf16), tails, preferred_element_type=f32)
    maxima, totals, gain = stats[:N_CTX], stats[N_CTX:2 * N_CTX], stats[2 * N_CTX:]
    factor = jnp.exp(maxima - jnp.max(maxima, axis=0, keepdims=True))
    factor = factor / jnp.sum(factor * totals, axis=0, keepdims=True)
    gt_ref[...] = jnp.concatenate([factor, jnp.zeros((ROWS - N_CTX, ROWS), f32)], axis=0).T
    mine = gt_ref[pl.ds(pl.multiple_of(core * 64, 64), 64), :]
    total = jnp.zeros((64, 128), f32)
    for s in range(N_CTX):
        total += mine[:, s:s + 1] * got_ref[s, :64, :].astype(f32)
    att_ref[core, chip] = total.astype(bf16)
    mine = att_ref.at[core, chip]

    for k in range(1, 16):
        remote(1, mine, mine, {"ctx": lax.rem(chip + k, 16) * 2 + core}).start()
    loads[0].wait()
    wait_all(recv_sem, 1, att_ref.at[core], 15)
    sibling = remote(2, att_ref.at[core], att_ref.at[core], {"ctx": ctx + 1 - 2 * core})
    sibling.start()

    def project(half):
        proj = jnp.zeros((64, 128), f32)
        for h in range(16):
            proj += jnp.dot(att_ref[half, h], wout_ref[h * 128:(h + 1) * 128, :], preferred_element_type=f32)
        zsum_ref[head, half] = proj.astype(bf16)
        send_heads(3, lambda to: zsum_ref.at[head, half], zsum_ref.at[head, half])
    project(core)
    sibling.wait()
    project(1 - core)
    wait_all(recv_sem, 3, zsum_ref, N_HEAD - 1)
    parts = [zsum_ref[z].astype(f32) for z in range(N_HEAD)]
    projected = (parts[0] + parts[1]) + (parts[2] + parts[3])
    residual = (resid_ref[...].astype(f32) + projected.reshape(ROWS, 128)).astype(bf16)
    res_ref[...] = residual.astype(f32)

    take_ref[...] = jnp.dot(sel_ref[...], residual, preferred_element_type=f32).astype(bf16).reshape(N_CTX, CAP, 128)
    send_all(4, lambda to: take_ref.at[to], taken_ref.at[ctx])
    taken_ref[ctx] = take_ref[ctx]
    loads[1].wait()
    loads[2].wait()
    loads[3].wait()
    wait_all(recv_sem, 4, taken_ref, N_CTX - 1)
    squares = jnp.zeros((CAP, 128), f32)
    for s in range(N_CTX):
        piece = taken_ref[s].astype(f32)
        squares += piece * piece
    scale = lax.rsqrt(jnp.sum(squares, axis=1, keepdims=True) * (1.0 / 4096) + 1e-6)
    for s in range(N_CTX):
        piece = taken_ref[s].astype(f32) * scale * gain[s:s + 1, :]
        xn_ref[s // 4, :, s % 4 * 128:s % 4 * 128 + 128] = piece.astype(bf16)

    def up_step(k, acc):
        rows = pl.ds(pl.multiple_of(k * 512, 512), 512)
        x = xn_ref[k]
        return (acc[0] + jnp.dot(x, wg_ref[rows, :], preferred_element_type=f32),
                acc[1] + jnp.dot(x, wu_ref[rows, :], preferred_element_type=f32))
    zero = jnp.zeros((CAP, 768), f32)
    gate, up = lax.fori_loop(0, 8, up_step, (zero, zero), unroll=4)
    hidden = (gate / (1.0 + jnp.exp(-gate)) * up).astype(bf16)

    def down_step(k, _):
        for u in range(2):
            n = lax.rem(ctx // 4 + 2 * k + u, 8)
            y = jnp.dot(hidden, wd_ref[:, pl.ds(pl.multiple_of(n * 512, 512), 512)], preferred_element_type=f32).astype(bf16)
            for q in range(4):
                eo_ref[n * 4 + q] = y[:, q * 128:(q + 1) * 128]
        for u in range(2):
            for q in range(4):
                to = lax.rem(ctx // 4 + 2 * k + u, 8) * 4 + q

                @pl.when(to != ctx)
                def _():
                    remote(5, eo_ref.at[to], eogot_ref.at[ctx], {"ctx": to}).start()
        return 0
    lax.fori_loop(0, 4, down_step, 0)
    eogot_ref[ctx] = eo_ref[ctx]
    wait_all(recv_sem, 5, eogot_ref, N_CTX - 1)
    outs = eogot_ref[...].reshape(N_CTX * CAP, 128)
    part = jnp.dot(wt_ref[...].reshape(3 * ROWS, N_CTX * CAP), outs, preferred_element_type=f32)
    part = part[:ROWS] + (part[ROWS:2 * ROWS] + part[2 * ROWS:])
    part_ref[...] = part.reshape(N_HEAD, 32, 128)
    send_heads(6, lambda to: part_ref.at[to], partgot_ref.at[head])
    partgot_ref[head] = part_ref[head]
    wait_all(recv_sem, 6, partgot_ref, N_HEAD - 1)
    mixture = (partgot_ref[0] + partgot_ref[1]) + (partgot_ref[2] + partgot_ref[3])
    own = res_ref[pl.ds(pl.multiple_of(head * 32, 32), 32), :]
    out_ref[...] = (own + mixture).astype(bf16)
    wait_all(send_sem, 0, msg_ref, N_CTX - 1)
    wait_all(send_sem, 1, att_ref.at[core], 15)
    wait_all(send_sem, 3, zsum_ref, N_HEAD - 1)
    wait_all(send_sem, 4, take_ref, N_CTX - 1)
    wait_all(send_sem, 5, eo_ref, N_CTX - 1)
    wait_all(send_sem, 6, part_ref, N_HEAD - 1)


def on_device(queries, key_codes, value_codes, key_book, value_book, lengths, resid, w_out, norm_gain,
              routes, route_weights, w_gate, w_up, w_down):
    vm = pl.BlockSpec(memory_space=pltpu.VMEM)
    hbm = pl.BlockSpec(memory_space=pl.ANY)
    V = pltpu.VMEM
    dma = pltpu.SemaphoreType.DMA
    return pl.pallas_call(
        layer_kernel,
        in_specs=[pl.BlockSpec(memory_space=pltpu.SMEM)] + [vm] * 7 + [hbm] * 6,
        out_specs=vm,
        out_shape=jax.ShapeDtypeStruct((32, 128), bf16),
        scratch_shapes=[
            V((ROWS, 8, 1024), i32), V((ROWS, 8, 1024), i32), V((16, 8, 128), i32), V((16, 8, 128), i32),
            V((2048, 128), bf16), V((2048, 128), bf16), V((SLOTS, 128, 1024), bf16), V((SLOTS, 128, 1024), bf16),
            V((2, 16, 128), f32), V((256, 256), bf16), V((N_CTX, 80, 128), bf16),
            V((2048, 128), bf16), V((4096, 768), bf16), V((4096, 768), bf16), V((768, 4096), bf16),
            V((N_CTX, 80, 128), bf16), V((2, 16, 64, 128), bf16), V((N_HEAD, 2, 64, 128), bf16),
            V((N_CTX, CAP, 128), bf16), V((N_CTX, CAP, 128), bf16), V((8, CAP, 512), bf16),
            V((N_CTX, CAP, 128), bf16), V((N_CTX, CAP, 128), bf16), V((N_HEAD, 32, 128), f32), V((N_HEAD, 32, 128), f32),
            V((ROWS, ROWS), f32), V((N_CTX * CAP, 128), bf16), V((N_CTX * CAP, 128), f32), V((3, ROWS, N_CTX * CAP), bf16),
            V((ROWS, 128), f32),
            dma((8,)), dma((8,)), dma((4,)), dma((7,)), dma((7,)),
        ],
        compiler_params=pltpu.CompilerParams(vmem_limit_bytes=58 << 20, collective_id=0, has_side_effects=True),
    )(lengths, queries.reshape(ROWS, 2048), jnp.transpose(key_book[0], (0, 2, 1)),
      jnp.transpose(value_book[0], (0, 2, 1)), norm_gain.reshape(1, 128), resid, routes.T, route_weights.T,
      key_codes, value_codes, w_out, w_gate, w_up, w_down)


def solution(mesh):
    return jax.shard_map(
        on_device,
        mesh=mesh,
        in_specs=(
            P(None, "head", None),
            P("head", None, None, "ctx"),
            P("head", None, None, "ctx"),
            P("head", None, None, None),
            P("head", None, None, None),
            P(),
            P(None, "ctx"),
            P("head", None, "ctx"),
            P("ctx"),
            P(),
            P(),
            P(("ctx", "head"), None, None),
            P(("ctx", "head"), None, None),
            P(("ctx", "head"), None, None),
        ),
        out_specs=P("head", "ctx"),
        check_vma=False,
    )
```

```python
import functools, math
import jax, jax.numpy as jnp
from jax import lax
from jax.experimental import pallas as pl
from jax.experimental.pallas import tpu as pltpu
from jax.sharding import PartitionSpec as P
LOG2E = 1.4426950408889634
f32, bf16, i32 = jnp.float32, jnp.bfloat16, jnp.int32
ROWS, CH, CAP, N_CTX, N_HEAD = 128, 16, 16, 32, 4
UNROLL, SLOTS, AHEAD = 16, 4, 2
MESH = pl.DeviceIdType.MESH


def hops(k):
    return min(k // 4, 4 - k // 4) + min(k % 4, 4 - k % 4)


CHIP_STEPS = sorted(range(1, 16), key=lambda k: (-hops(k), k))
CTX_STEPS = sorted(range(1, N_CTX), key=lambda k: (-hops(k // 2), k))
HEAD_STEPS = (2, 1, 3)

def pow2_scale(x):
    sc = jnp.ones_like(x)
    for p in (32, 16, 8, 4, 2, 1):
        f = float(2.0 ** p)
        ok = x * f <= 4.0
        x = jnp.where(ok, x * f, x)
        sc = jnp.where(ok, sc * f, sc)
    return sc

def build_table(book_ref, table_ref, turn):
    rows = jnp.dot(turn, book_ref[...].reshape(128, 256), preferred_element_type=f32)
    entries = [rows[8 * d:8 * d + 8] for d in range(16)]
    top = jnp.abs(entries[0])
    for d in range(1, 16):
        top = jnp.maximum(top, jnp.abs(entries[d]))
    sc = pow2_scale(jnp.max(top, axis=1, keepdims=True))
    for p in range(8):
        hi = jnp.round(entries[2 * p] * (sc * 4096.0)).astype(i32)
        lo = jnp.round(entries[2 * p + 1] * (sc * 4096.0)).astype(i32)
        word = hi * 65536 + lo
        table_ref[2 * p] = word[:, :128]
        table_ref[2 * p + 1] = word[:, 128:]
    inv = 1.0 / sc * (2.0 ** -28)
    lane = lax.broadcasted_iota(i32, (8, 128), 1)
    sub = lax.broadcasted_iota(i32, (8, 128), 0)
    return jnp.sum(jnp.where(lane % 8 == sub, inv, 0.0), axis=0, keepdims=True)

def layer_kernel(len_ref, q_ref, kb_ref, vb_ref, gain_ref, resid_ref, routes_ref, rw_ref,
                 kc_hbm, vc_hbm, wout_hbm, wg_hbm, wu_hbm, wd_hbm,
                 out_ref,
                 kc_ref, vc_ref, kt_ref, vt_ref, qp_ref, ox_ref, key_ref, val_ref, ml_ref, swap_ref, msg_ref,
                 wout_ref, wg_ref, wu_ref, wd_ref, got_ref, att_ref, zsum_ref, take_ref, taken_ref, xn_ref,
                 eo_ref, eogot_ref, part_ref, partgot_ref, gt_ref, sel_ref, selw_ref, wt_ref, res_ref,
                 ksem, vsem, load_sem, send_sem, recv_sem):
    ctx = lax.axis_index("ctx")
    head = lax.axis_index("head")
    core = lax.rem(ctx, 2)
    chip = ctx // 2
    barrier = pltpu.get_barrier_semaphore()

    def greet_ctx(k, _):
        pl.semaphore_signal(barrier, inc=1, device_id={"ctx": lax.rem(ctx + k, N_CTX)}, device_id_type=MESH)
        return 0
    lax.fori_loop(1, N_CTX, greet_ctx, 0)
    for k in range(1, N_HEAD):
        pl.semaphore_signal(barrier, inc=1, device_id={"head": lax.rem(head + k, N_HEAD)}, device_id_type=MESH)

    def code_copy(c, hbm, vmem, sem):
        at = pl.ds(c * CH, CH)
        return pltpu.make_async_copy(hbm.at[0, at], vmem.at[at], sem.at[c])
    for c in range(ROWS // CH):
        code_copy(c, kc_hbm, kc_ref, ksem).start()
        code_copy(c, vc_hbm, vc_ref, vsem).start()
    loads = [pltpu.make_async_copy(wout_hbm.at[0], wout_ref, load_sem.at[0]),
             pltpu.make_async_copy(wg_hbm.at[0], wg_ref, load_sem.at[1]),
             pltpu.make_async_copy(wu_hbm.at[0], wu_ref, load_sem.at[2]),
             pltpu.make_async_copy(wd_hbm.at[0], wd_ref, load_sem.at[3])]
    for load in loads:
        load.start()

    offset = ctx * 1024
    i = lax.broadcasted_iota(i32, (128, 128), 0)
    j = lax.broadcasted_iota(i32, (128, 128), 1)
    to_ds = (i // 16 == j % 8) & (i % 16 == j // 8)
    to_sd = (j // 16 == i % 8) & (j % 16 == i // 8)
    perm = jnp.where(to_sd, 1.0, 0.0).astype(bf16)
    k_inv = build_table(kb_ref, kt_ref, perm)
    v_inv = build_table(vb_ref, vt_ref, perm)
    ml_ref[...] = jnp.zeros_like(ml_ref)
    ox_ref[...] = jnp.zeros_like(ox_ref)
    r = lax.broadcasted_iota(i32, (256, 256), 0)
    c = lax.broadcasted_iota(i32, (256, 256), 1)
    swap_ref[...] = ((r // 16 == c % 16) & (r % 16 == c // 16)).astype(f32).astype(bf16)
    k_perm = jnp.where(to_ds, k_inv, 0.0).astype(bf16)

    def turn_queries(c, part):
        x = q_ref[pl.ds(pl.multiple_of(c * CH, CH), CH), :]
        x = jnp.concatenate([x[:, h * 128:(h + 1) * 128] for h in range(16)], axis=0)
        half = pl.multiple_of(part * 128, 128)
        x = jnp.dot(swap_ref[pl.ds(half, 128), :], x, preferred_element_type=f32).astype(bf16)
        at = pl.ds(pl.multiple_of(c * 256 + half, 128), 128)
        qp_ref[at, :] = jnp.dot(x, k_perm, preferred_element_type=f32).astype(bf16)
    turn_queries(0, 0)
    turn_queries(0, 1)
    lane = lax.broadcasted_iota(i32, (16, 128), 1)
    pos = lax.broadcasted_iota(i32, (16, 1024), 1)
    C = 1.0 / math.sqrt(128.0)

    def three(x):
        hi = x.astype(bf16)
        rest = x - hi.astype(f32)
        mid = rest.astype(bf16)
        return hi, mid, (rest - mid.astype(f32)).astype(bf16)

    def dequant(codes_ref, b, table_ref, dst_ref, slot):
        for j in range(8):
            at = slice(j * 128, (j + 1) * 128)
            idx = codes_ref[b, :, at]
            low = idx & 127
            upper = idx > 127
            for p in range(8):
                w0 = jnp.take_along_axis(table_ref[2 * p], low, axis=1, mode="promise_in_bounds")
                w1 = jnp.take_along_axis(table_ref[2 * p + 1], low, axis=1, mode="promise_in_bounds")
                w = jnp.where(upper, w1, w0)
                pair = jnp.concatenate([w.astype(f32), (w << 16).astype(f32)], axis=0)
                dst_ref[slot, p * 16:(p + 1) * 16, at] = pair.astype(bf16)

    def fetch(b, slot):
        dequant(kc_ref, b, kt_ref, key_ref, slot)
        dequant(vc_ref, b, vt_ref, val_ref, slot)

    def row(b, slot):
        at = pl.ds(pl.multiple_of(b * 16, 16), 16)
        raw = jnp.dot(qp_ref[at, :], key_ref[slot], preferred_element_type=f32)
        vis = pos < len_ref[b] - offset
        raw = jnp.where(vis, raw, -1e30)
        top = raw[:, 0:128]
        for k in range(1, 8):
            top = jnp.maximum(top, raw[:, k * 128:(k + 1) * 128])
        top = jnp.max(top.astype(bf16), axis=1, keepdims=True).astype(f32)
        w = jnp.where(vis, jnp.exp2((raw - top) * (C * LOG2E)), 0.0)
        tot = w[:, 0:128]
        for k in range(1, 8):
            tot = tot + w[:, k * 128:(k + 1) * 128]
        tot = jnp.dot(jnp.concatenate(three(tot), axis=1), jnp.ones((384, 128), bf16), preferred_element_type=f32)
        out = lax.dot_general(w.astype(bf16), val_ref[slot], (((1,), (1,)), ((), ())), preferred_element_type=f32)
        ox_ref[at, :] = (out * v_inv).astype(bf16)
        here = lane == b
        ml_ref[0] = jnp.where(here, top * C, ml_ref[0])
        ml_ref[1] = jnp.where(here, tot, ml_ref[1])

    def turn(c, part):
        y = jnp.dot(swap_ref[pl.ds(pl.multiple_of(part * 128, 128), 128), :],
                    ox_ref[pl.ds(pl.multiple_of(c * 256, 256), 256), :], preferred_element_type=f32).astype(bf16)
        y = jnp.dot(y, perm, preferred_element_type=f32).astype(bf16)
        at = pl.ds(pl.multiple_of(lax.rem(c, 4) * 16, 16), 16)
        for h in range(8):
            msg_ref[(part * 8 + h) * 2 + c // 4, at, :] = y[h * 16:(h + 1) * 16]

    def add_tail(half):
        pieces = [x.astype(f32) for x in three(ml_ref[0]) + three(ml_ref[1])]
        line = lax.broadcasted_iota(i32, (16, 128), 0)
        gain = jnp.where(line == 6, gain_ref[...].astype(f32), 0.0)
        for h in range(16):
            tail = gain
            for k in range(6):
                tail = jnp.where(line == k, pieces[k][h:h + 1, :], tail)
            msg_ref[2 * h + half, 64:80, :] = tail.astype(bf16)

    def remote(phase, src, dst, to):
        return pltpu.make_async_remote_copy(
            src_ref=src, dst_ref=dst, send_sem=send_sem.at[phase], recv_sem=recv_sem.at[phase],
            device_id=to, device_id_type=MESH)

    def send_quarter(q):
        half = q // 2
        rows = pl.ds(0, 32) if q % 2 == 0 else pl.ds(32, 48)

        for k in CHIP_STEPS:
            to = lax.rem(chip + k, 16) * 2 + half
            remote(0, msg_ref.at[to, rows], got_ref.at[ctx, rows], {"ctx": to}).start()

        @pl.when(core != half)
        def _():
            to = chip * 2 + half
            remote(0, msg_ref.at[to, rows], got_ref.at[ctx, rows], {"ctx": to}).start()

    def send_all(phase, source, target):
        for k in CTX_STEPS:
            to = lax.rem(ctx + k, N_CTX)
            remote(phase, source(to), target, {"ctx": to}).start()

    def wait_all(sems, phase, ref, count):
        view = ref.at[pl.ds(0, count)]
        pltpu.make_async_copy(view, view, sems.at[phase]).wait()

    def send_heads(phase, source, target):
        for k in HEAD_STEPS:
            to = lax.rem(head + k, N_HEAD)
            remote(phase, source(to), target, {"head": to}).start()

    def wait_chunk(c):
        code_copy(c, kc_hbm, kc_ref, ksem).wait()
        code_copy(c, vc_hbm, vc_ref, vsem).wait()
    wait_chunk(0)
    for b in range(AHEAD):
        fetch(b, b)
    pl.semaphore_wait(barrier, N_CTX - 1 + N_HEAD - 1)

    def chunk(c, _):
        @pl.when(c < ROWS // CH - 1)
        def _():
            wait_chunk(c + 1)

        def body(i, _):
            b = c * CH + i * UNROLL
            for part in range(2) if UNROLL == CH else (i,):
                turn(jnp.maximum(c - 1, 0), part)
                turn_queries(jnp.minimum(c + 1, ROWS // CH - 1), part)
            for u in range(UNROLL):
                fetch(jnp.minimum(b + u + AHEAD, ROWS - 1), (u + AHEAD) % SLOTS)
                row(b + u, u % SLOTS)
            return 0
        lax.fori_loop(0, CH // UNROLL, body, 0)
        for q in range(3):
            @pl.when(c == 2 * q + 2)
            def _():
                if q == 1:
                    add_tail(0)
                send_quarter(q)
        return 0
    lax.fori_loop(0, ROWS // CH, chunk, 0)
    turn(ROWS // CH - 1, 0)
    turn(ROWS // CH - 1, 1)
    add_tail(1)
    send_quarter(3)
    got_ref[ctx] = msg_ref[ctx]

    names, shares = routes_ref[...], rw_ref[...]
    expert = lax.broadcasted_iota(i32, (N_CTX, ROWS), 0) * N_HEAD + head
    member = jnp.zeros((N_CTX, ROWS), f32)
    weight = jnp.zeros((N_CTX, ROWS), f32)
    for k in range(8):
        same = names[k:k + 1, :] == expert
        member = jnp.where(same, 1.0, member)
        weight = jnp.where(same, shares[k:k + 1, :], weight)
    before = (lax.broadcasted_iota(i32, (ROWS, ROWS), 0) < lax.broadcasted_iota(i32, (ROWS, ROWS), 1)).astype(f32).astype(bf16)
    slot = jnp.dot(member.astype(bf16), before, preferred_element_type=f32).astype(i32)
    slot = jnp.where(member > 0.5, slot, -1)
    slots = lax.broadcasted_iota(i32, (CAP, ROWS), 0)
    for e in range(N_CTX):
        hit = slot[e:e + 1, :] == slots
        sel_ref[e * CAP:(e + 1) * CAP, :] = jnp.where(hit, 1.0, 0.0).astype(bf16)
        selw_ref[e * CAP:(e + 1) * CAP, :] = jnp.where(hit, weight[e:e + 1, :], 0.0)
    for t in range(N_CTX * CAP // 128):
        block = selw_ref[t * 128:(t + 1) * 128, :].T
        hi = block.astype(bf16)
        rest = block - hi.astype(f32)
        mid = rest.astype(bf16)
        wt_ref[0, :, t * 128:(t + 1) * 128] = hi
        wt_ref[1, :, t * 128:(t + 1) * 128] = mid
        wt_ref[2, :, t * 128:(t + 1) * 128] = (rest - mid.astype(f32)).astype(bf16)

    wait_all(recv_sem, 0, got_ref, N_CTX - 1)
    tails = got_ref[:, 64:80, :].reshape(N_CTX * 16, 128)
    r = lax.broadcasted_iota(i32, (3 * N_CTX, N_CTX * 16), 0)
    c = lax.broadcasted_iota(i32, (3 * N_CTX, N_CTX * 16), 1)
    kind, at = r // N_CTX, c % 16
    wanted = (c // 16 == r % N_CTX) & (at // 3 == kind) & (at < 7)
    stats = jnp.dot(jnp.where(wanted, 1.0, 0.0).astype(bf16), tails, preferred_element_type=f32)
    maxima, totals, gain = stats[:N_CTX], stats[N_CTX:2 * N_CTX], stats[2 * N_CTX:]
    factor = jnp.exp(maxima - jnp.max(maxima, axis=0, keepdims=True))
    factor = factor / jnp.sum(factor * totals, axis=0, keepdims=True)
    gt_ref[...] = jnp.concatenate([factor, jnp.zeros((ROWS - N_CTX, ROWS), f32)], axis=0).T
    mine = gt_ref[pl.ds(pl.multiple_of(core * 64, 64), 64), :]
    total = jnp.zeros((64, 128), f32)
    for s in range(N_CTX):
        total += mine[:, s:s + 1] * got_ref[s, :64, :].astype(f32)
    att_ref[core, chip] = total.astype(bf16)
    mine = att_ref.at[core, chip]

    for k in CHIP_STEPS:
        remote(1, mine, mine, {"ctx": lax.rem(chip + k, 16) * 2 + core}).start()
    loads[0].wait()
    wait_all(recv_sem, 1, att_ref.at[core], 15)
    sibling = remote(2, att_ref.at[core], att_ref.at[core], {"ctx": ctx + 1 - 2 * core})
    sibling.start()

    def project(half):
        proj = jnp.zeros((64, 128), f32)
        for h in range(16):
            proj += jnp.dot(att_ref[half, h], wout_ref[h * 128:(h + 1) * 128, :], preferred_element_type=f32)
        zsum_ref[head, half] = proj.astype(bf16)
        send_heads(3, lambda to: zsum_ref.at[head, half], zsum_ref.at[head, half])
    project(core)
    sibling.wait()
    project(1 - core)
    wait_all(recv_sem, 3, zsum_ref, N_HEAD - 1)
    parts = [zsum_ref[z].astype(f32) for z in range(N_HEAD)]
    projected = (parts[0] + parts[1]) + (parts[2] + parts[3])
    residual = (resid_ref[...].astype(f32) + projected.reshape(ROWS, 128)).astype(bf16)
    res_ref[...] = residual.astype(f32)

    take_ref[...] = jnp.dot(sel_ref[...], residual, preferred_element_type=f32).astype(bf16).reshape(N_CTX, CAP, 128)
    send_all(4, lambda to: take_ref.at[to], taken_ref.at[ctx])
    taken_ref[ctx] = take_ref[ctx]
    loads[1].wait()
    loads[2].wait()
    loads[3].wait()
    wait_all(recv_sem, 4, taken_ref, N_CTX - 1)
    squares = jnp.zeros((CAP, 128), f32)
    for s in range(N_CTX):
        piece = taken_ref[s].astype(f32)
        squares += piece * piece
    scale = lax.rsqrt(jnp.sum(squares, axis=1, keepdims=True) * (1.0 / 4096) + 1e-6)
    for s in range(N_CTX):
        piece = taken_ref[s].astype(f32) * scale * gain[s:s + 1, :]
        xn_ref[s // 4, :, s % 4 * 128:s % 4 * 128 + 128] = piece.astype(bf16)

    def up_step(k, acc):
        rows = pl.ds(pl.multiple_of(k * 512, 512), 512)
        x = xn_ref[k]
        return (acc[0] + jnp.dot(x, wg_ref[rows, :], preferred_element_type=f32),
                acc[1] + jnp.dot(x, wu_ref[rows, :], preferred_element_type=f32))
    zero = jnp.zeros((CAP, 768), f32)
    gate, up = lax.fori_loop(0, 8, up_step, (zero, zero), unroll=4)
    hidden = (gate / (1.0 + jnp.exp(-gate)) * up).astype(bf16)

    def down_step(k, _):
        for u in range(2):
            n = lax.rem(ctx // 4 + 3 + 2 * k + u, 8)
            y = jnp.dot(hidden, wd_ref[:, pl.ds(pl.multiple_of(n * 512, 512), 512)], preferred_element_type=f32).astype(bf16)
            for q in range(4):
                eo_ref[n * 4 + q] = y[:, q * 128:(q + 1) * 128]
        for u in range(2):
            for q in range(4):
                to = lax.rem(ctx // 4 + 3 + 2 * k + u, 8) * 4 + q

                @pl.when(to != ctx)
                def _():
                    remote(5, eo_ref.at[to], eogot_ref.at[ctx], {"ctx": to}).start()
        return 0
    lax.fori_loop(0, 4, down_step, 0)
    eogot_ref[ctx] = eo_ref[ctx]
    wait_all(recv_sem, 5, eogot_ref, N_CTX - 1)
    outs = eogot_ref[...].reshape(N_CTX * CAP, 128)
    part = jnp.dot(wt_ref[...].reshape(3 * ROWS, N_CTX * CAP), outs, preferred_element_type=f32)
    part = part[:ROWS] + (part[ROWS:2 * ROWS] + part[2 * ROWS:])
    part_ref[...] = part.reshape(N_HEAD, 32, 128)
    send_heads(6, lambda to: part_ref.at[to], partgot_ref.at[head])
    partgot_ref[head] = part_ref[head]
    wait_all(recv_sem, 6, partgot_ref, N_HEAD - 1)
    mixture = (partgot_ref[0] + partgot_ref[1]) + (partgot_ref[2] + partgot_ref[3])
    own = res_ref[pl.ds(pl.multiple_of(head * 32, 32), 32), :]
    out_ref[...] = (own + mixture).astype(bf16)
    wait_all(send_sem, 0, msg_ref, N_CTX - 1)
    wait_all(send_sem, 1, att_ref.at[core], 15)
    wait_all(send_sem, 3, zsum_ref, N_HEAD - 1)
    wait_all(send_sem, 4, take_ref, N_CTX - 1)
    wait_all(send_sem, 5, eo_ref, N_CTX - 1)
    wait_all(send_sem, 6, part_ref, N_HEAD - 1)


def on_device(queries, key_codes, value_codes, key_book, value_book, lengths, resid, w_out, norm_gain,
              routes, route_weights, w_gate, w_up, w_down):
    vm = pl.BlockSpec(memory_space=pltpu.VMEM)
    hbm = pl.BlockSpec(memory_space=pl.ANY)
    V = pltpu.VMEM
    dma = pltpu.SemaphoreType.DMA
    return pl.pallas_call(
        layer_kernel,
        in_specs=[pl.BlockSpec(memory_space=pltpu.SMEM)] + [vm] * 7 + [hbm] * 6,
        out_specs=vm,
        out_shape=jax.ShapeDtypeStruct((32, 128), bf16),
        scratch_shapes=[
            V((ROWS, 8, 1024), i32), V((ROWS, 8, 1024), i32), V((16, 8, 128), i32), V((16, 8, 128), i32),
            V((2048, 128), bf16), V((2048, 128), bf16), V((SLOTS, 128, 1024), bf16), V((SLOTS, 128, 1024), bf16),
            V((2, 16, 128), f32), V((256, 256), bf16), V((N_CTX, 80, 128), bf16),
            V((2048, 128), bf16), V((4096, 768), bf16), V((4096, 768), bf16), V((768, 4096), bf16),
            V((N_CTX, 80, 128), bf16), V((2, 16, 64, 128), bf16), V((N_HEAD, 2, 64, 128), bf16),
            V((N_CTX, CAP, 128), bf16), V((N_CTX, CAP, 128), bf16), V((8, CAP, 512), bf16),
            V((N_CTX, CAP, 128), bf16), V((N_CTX, CAP, 128), bf16), V((N_HEAD, 32, 128), f32), V((N_HEAD, 32, 128), f32),
            V((ROWS, ROWS), f32), V((N_CTX * CAP, 128), bf16), V((N_CTX * CAP, 128), f32), V((3, ROWS, N_CTX * CAP), bf16),
            V((ROWS, 128), f32),
            dma((8,)), dma((8,)), dma((4,)), dma((7,)), dma((7,)),
        ],
        compiler_params=pltpu.CompilerParams(vmem_limit_bytes=58 << 20, collective_id=0, has_side_effects=True),
    )(lengths, queries.reshape(ROWS, 2048), jnp.transpose(key_book[0], (0, 2, 1)),
      jnp.transpose(value_book[0], (0, 2, 1)), norm_gain.reshape(1, 128), resid, routes.T, route_weights.T,
      key_codes, value_codes, w_out, w_gate, w_up, w_down)


def solution(mesh):
    return jax.shard_map(
        on_device,
        mesh=mesh,
        in_specs=(
            P(None, "head", None),
            P("head", None, None, "ctx"),
            P("head", None, None, "ctx"),
            P("head", None, None, None),
            P("head", None, None, None),
            P(),
            P(None, "ctx"),
            P("head", None, "ctx"),
            P("ctx"),
            P(),
            P(),
            P(("ctx", "head"), None, None),
            P(("ctx", "head"), None, None),
            P(("ctx", "head"), None, None),
        ),
        out_specs=P("head", "ctx"),
        check_vma=False,
    )
```
